32 devices in a mesh: ctx: 8 (over z, x), ch: 4 (over y, core).
Axes of the slice: x: 2, y: 2, z: 4, core: 2. Of those that a mesh axis runs over, the one named last changes fastest.
Arguments:
- query_gate: bfloat16 [4096, 4096], P('ctx', 'ch'), may hold values from -6 to 6
- key_gate: bfloat16 [4096, 4096], P('ctx', 'ch'), may hold values from -6 to 6
- value_in: bfloat16 [4096, 4096], P('ctx', 'ch'), may hold values from -6 to 6
- filter_taps: float32 [4096, 4096], P(None, 'ch'), may hold values from -0.09375 to 0.09375
- skip_gain: float32 [4096], P('ch'), may hold values from -4 to 4
- out_weight: bfloat16 [4096, 4096], P('ch'), may hold values from -0.09375 to 0.09375
Outputs:
- mixed_out: bfloat16 [4096, 4096], P('ctx', 'ch')
The draws below stay inside these ranges and needn't reach their ends.
All inputs are finite; a program needn't handle non-finite values.
Results may differ from the reference program's by a relative error of at most 0.017.
Values may be sent and summed in bfloat16 or wider, within the bound.
A program may use at most 192 MiB of HBM per device.

```python
import jax
import jax.numpy as jnp
from jax import lax

D = 4096
SPAN = 512
WIN = 8
SEQ = 4096
N_CTX = 8


def levels(rng, shape, shards, smallest, largest):
    level, own = 1.0, jax.random.fold_in(rng, 6)
    for dim, shards_of in shards:
        draws = jnp.exp(jax.random.uniform(jax.random.fold_in(own, dim), (shards_of,), jnp.float32, smallest / len(shards), largest / len(shards)))
        level = level * jnp.repeat(draws, shape[dim] // shards_of).reshape([-1 if axis == dim else 1 for axis in range(len(shape))])
    return level


def noise(rng, extent, deviation, bound, pieces=(), held_as=jnp.bfloat16):
    entries = jax.random.normal(rng, extent, jnp.float32) * deviation
    if len(pieces) > 0:
        entries = levels(rng, extent, pieces, -0.22, 0.18) * entries
    return jnp.clip(entries, min=-bound, max=bound).astype(held_as)


def setup_inputs(seed: int = 0) -> dict:
    arg_keys = jax.random.split(jax.random.key(seed), 7)
    query_gate = noise(arg_keys[0], (SEQ, D), 1.0, 6.0, ((0, 8), (1, 4)))
    key_gate = noise(arg_keys[1], (SEQ, D), 1.0, 6.0, ((0, 8), (1, 4)))
    value_in = noise(arg_keys[2], (SEQ, D), 1.0, 6.0, ((0, 8), (1, 4)))
    filter_taps = noise(arg_keys[3], (WIN * SPAN, D), (WIN * SPAN) ** -0.5, 0.09375, ((1, 4),), jnp.float32)
    skip_gain = noise(arg_keys[4], (D,), 1.0, 4.0, ((0, 4),), jnp.float32)
    out_weight = noise(arg_keys[5], (D, D), D ** -0.5, 0.09375, ((0, 4),))
    return dict(query_gate=query_gate, key_gate=key_gate, value_in=value_in, filter_taps=filter_taps, skip_gain=skip_gain, out_weight=out_weight)


def reference(query_gate, key_gate, value_in, filter_taps, skip_gain, out_weight):
    mixed_in = (key_gate.astype(jnp.float32) * value_in.astype(jnp.float32)).astype(jnp.bfloat16)
    spans = mixed_in.astype(jnp.float32).reshape(N_CTX, SPAN, D)
    spectra = jnp.fft.rfft(spans, n=2 * SPAN, axis=1)
    real_part = lax.optimization_barrier(jnp.real(spectra).astype(jnp.bfloat16)).astype(jnp.float32)
    imag_part = lax.optimization_barrier(jnp.imag(spectra).astype(jnp.bfloat16)).astype(jnp.float32)
    padded_taps = jnp.concatenate([jnp.zeros((SPAN, D), jnp.float32), filter_taps, jnp.zeros((SPAN, D), jnp.float32)], axis=0)
    leading = jnp.zeros((WIN, SPAN + 1, D), jnp.float32)
    real_padded = jnp.concatenate([leading, real_part], axis=0)
    imag_padded = jnp.concatenate([leading, imag_part], axis=0)
    total_real = jnp.zeros((N_CTX, SPAN + 1, D), jnp.float32)
    total_imag = jnp.zeros((N_CTX, SPAN + 1, D), jnp.float32)
    for lag_index in range(WIN + 1):
        window = padded_taps[lag_index * SPAN: lag_index * SPAN + 2 * SPAN]
        kernel = jnp.fft.rfft(window, axis=0)
        kernel_real = jnp.real(kernel)[None]
        kernel_imag = jnp.imag(kernel)[None]
        shifted_real = real_padded[WIN - lag_index: WIN - lag_index + N_CTX]
        shifted_imag = imag_padded[WIN - lag_index: WIN - lag_index + N_CTX]
        total_real = total_real + kernel_real * shifted_real - kernel_imag * shifted_imag
        total_imag = total_imag + kernel_real * shifted_imag + kernel_imag * shifted_real
    signal = jnp.fft.irfft(lax.complex(total_real, total_imag), n=2 * SPAN, axis=1)
    conv_out = signal[:, SPAN:, :].reshape(SEQ, D)
    combined = conv_out + skip_gain[None, :] * mixed_in.astype(jnp.float32)
    gated = (query_gate.astype(jnp.float32) * combined).astype(jnp.bfloat16)
    return jnp.dot(gated, out_weight, preferred_element_type=jnp.float32).astype(jnp.bfloat16)
```

```python
import ml_dtypes
import numpy as np

import jax
import jax.numpy as jnp
from jax import lax
from jax.sharding import PartitionSpec as P

BF16 = jnp.bfloat16
F32 = jnp.float32


def transform_tables(length):
    freqs = np.concatenate([np.arange(0, length, 2), np.arange(1, length, 2)])[:, None]
    times = np.arange(length)[None, :]
    angle = (freqs * times % (2 * length)) * (np.pi / length)
    real, imag = np.cos(angle), -np.sin(angle)
    imag[0] = 1.0 - 2.0 * (np.arange(length) % 2)
    forward = np.concatenate([real, imag], axis=0)
    angle = (freqs * (times + length) % (2 * length)) * (np.pi / length)
    real, imag = np.cos(angle) / length, -np.sin(angle) / length
    real[0] = 0.5 / length
    imag[0] = (1.0 - 2.0 * ((np.arange(length) + length) % 2)) * 0.5 / length
    inverse = np.concatenate([real, imag], axis=0).T
    return forward.astype(ml_dtypes.bfloat16), inverse.astype(ml_dtypes.bfloat16)


def long_conv(x, taps, forward, inverse):
    spans, length, _ = x.shape
    win = taps.shape[0]
    data = jnp.einsum("mn,knc->kmc", forward, x, preferred_element_type=F32)
    block = jnp.einsum("mn,knc->kmc", forward, taps, preferred_element_type=F32)
    parity = jnp.where(jnp.arange(2 * length) % length < length // 2, 1.0, -1.0)[None, :, None]
    before = jnp.concatenate([jnp.zeros_like(data[:1]), data[:-1]], axis=0)
    pair = before + parity * data
    edge = (jnp.arange(length) == 0)[None, :, None]
    real = jnp.zeros_like(data[:, :length])
    imag = jnp.zeros_like(real)
    for lag in range(min(win, spans)):
        own = jnp.concatenate([jnp.zeros_like(pair[:lag]), pair[: spans - lag]], axis=0)
        own_real, own_imag = own[:, :length], own[:, length:]
        tap_real, tap_imag = block[lag, :length][None], block[lag, length:][None]
        first, second = tap_real * own_real, tap_imag * own_imag
        real = real + jnp.where(edge, first, first - second)
        imag = imag + jnp.where(edge, second, tap_real * own_imag + tap_imag * own_real)
    total = jnp.concatenate([real, imag], axis=1).astype(BF16)
    return jnp.einsum("im,kmc->kic", inverse, total, preferred_element_type=F32)


def plain_body(forward, inverse, query_gate, key_gate, value_in, filter_taps, skip_gain, out_weight):
    length, width = query_gate.shape
    devices = lax.axis_size("ctx")
    share = width // devices
    mixed_in = (key_gate.astype(F32) * value_in.astype(F32)).astype(BF16)
    x = lax.all_to_all(mixed_in, "ctx", split_axis=1, concat_axis=0, tiled=True)
    taps = lax.dynamic_slice_in_dim(filter_taps, lax.axis_index("ctx") * share, share, axis=1)
    conv = long_conv(
        x.reshape(devices, length, share),
        taps.astype(BF16).reshape(-1, length, share),
        forward,
        inverse,
    )
    conv = conv.astype(BF16).reshape(devices * length, share)
    conv = lax.all_to_all(conv, "ctx", split_axis=0, concat_axis=1, tiled=True)
    combined = conv.astype(F32) + skip_gain[None, :] * mixed_in.astype(F32)
    gated = (query_gate.astype(F32) * combined).astype(BF16)
    partial_value = jnp.dot(gated, out_weight, preferred_element_type=F32)
    return lax.psum_scatter(partial_value.astype(BF16), "ch", scatter_dimension=1, tiled=True)


def solution(mesh):
    in_specs = (
        P("ctx", "ch"),
        P("ctx", "ch"),
        P("ctx", "ch"),
        P(None, "ch"),
        P("ch"),
        P("ch", None),
    )
    out_specs = P("ctx", "ch")

    def whole(query_gate, *rest):
        length = query_gate.shape[0] // mesh.shape["ctx"]
        forward, inverse = transform_tables(length)

        def body(*args):
            return plain_body(forward, inverse, *args)

        return jax.shard_map(
            body, mesh=mesh, in_specs=in_specs, out_specs=out_specs, check_vma=False
        )(query_gate, *rest)

    return whole
```

```python
import functools

import ml_dtypes
import numpy as np

import jax
import jax.numpy as jnp
from jax import lax
from jax.experimental import pallas as pl
from jax.experimental.pallas import tpu as pltpu
from jax.sharding import PartitionSpec as P

BF16 = jnp.bfloat16
F32 = jnp.float32


def transform_tables(length):
    freqs = np.concatenate([np.arange(0, length, 2), np.arange(1, length, 2)])[:, None]
    times = np.arange(length)[None, :]
    angle = (freqs * times % (2 * length)) * (np.pi / length)
    real, imag = np.cos(angle), -np.sin(angle)
    imag[0] = 1.0 - 2.0 * (np.arange(length) % 2)
    forward = np.concatenate([real, imag], axis=0)
    angle = (freqs * (times + length) % (2 * length)) * (np.pi / length)
    real, imag = np.cos(angle) / length, -np.sin(angle) / length
    real[0] = 0.5 / length
    imag[0] = (1.0 - 2.0 * ((np.arange(length) + length) % 2)) * 0.5 / length
    inverse = np.concatenate([real, imag], axis=0).T
    return forward.astype(ml_dtypes.bfloat16), inverse.astype(ml_dtypes.bfloat16)


def long_conv(x, taps, forward, inverse):
    spans, length, _ = x.shape
    win = taps.shape[0]
    data = jnp.einsum("mn,knc->kmc", forward, x, preferred_element_type=F32)
    block = jnp.einsum("mn,knc->kmc", forward, taps, preferred_element_type=F32)
    parity = jnp.where(jnp.arange(2 * length) % length < length // 2, 1.0, -1.0)[None, :, None]
    before = jnp.concatenate([jnp.zeros_like(data[:1]), data[:-1]], axis=0)
    pair = before + parity * data
    edge = (jnp.arange(length) == 0)[None, :, None]
    real = jnp.zeros_like(data[:, :length])
    imag = jnp.zeros_like(real)
    for lag in range(min(win, spans)):
        own = jnp.concatenate([jnp.zeros_like(pair[:lag]), pair[: spans - lag]], axis=0)
        own_real, own_imag = own[:, :length], own[:, length:]
        tap_real, tap_imag = block[lag, :length][None], block[lag, length:][None]
        first, second = tap_real * own_real, tap_imag * own_imag
        real = real + jnp.where(edge, first, first - second)
        imag = imag + jnp.where(edge, second, tap_real * own_imag + tap_imag * own_real)
    total = jnp.concatenate([real, imag], axis=1).astype(BF16)
    return jnp.einsum("im,kmc->kic", inverse, total, preferred_element_type=F32)


def plain_body(forward, inverse, query_gate, key_gate, value_in, filter_taps, skip_gain, out_weight):
    length, width = query_gate.shape
    devices = lax.axis_size("ctx")
    share = width // devices
    mixed_in = (key_gate.astype(F32) * value_in.astype(F32)).astype(BF16)
    x = lax.all_to_all(mixed_in, "ctx", split_axis=1, concat_axis=0, tiled=True)
    taps = lax.dynamic_slice_in_dim(filter_taps, lax.axis_index("ctx") * share, share, axis=1)
    conv = long_conv(
        x.reshape(devices, length, share),
        taps.astype(BF16).reshape(-1, length, share),
        forward,
        inverse,
    )
    conv = conv.astype(BF16).reshape(devices * length, share)
    conv = lax.all_to_all(conv, "ctx", split_axis=0, concat_axis=1, tiled=True)
    combined = conv.astype(F32) + skip_gain[None, :] * mixed_in.astype(F32)
    gated = (query_gate.astype(F32) * combined).astype(BF16)
    partial_value = jnp.dot(gated, out_weight, preferred_element_type=F32)
    return lax.psum_scatter(partial_value.astype(BF16), "ch", scatter_dimension=1, tiled=True)


MESH = pl.DeviceIdType.MESH
CHUNKS = 4
ROWS = 8


def spectral_tile(row, sign, edge, taps_ref, data_ref, total_ref):
    pairs, height, lanes = data_ref.shape
    share, spans = lanes // 2, 2 * pairs
    real_rows, imag_rows = pl.ds(row, ROWS), pl.ds(row + height // 2, ROWS)

    def parts(ref, index):
        cols = slice((index % 2) * share, (index % 2 + 1) * share)
        return ref[index // 2, real_rows, cols], ref[index // 2, imag_rows, cols]

    taps = [parts(taps_ref, j) for j in range(2 * taps_ref.shape[0])]
    own, before = [], None
    for span in range(spans):
        here = parts(data_ref, span)
        if before is None:
            own.append(here if sign > 0 else tuple(-part for part in here))
        elif sign > 0:
            own.append(tuple(b + h for b, h in zip(before, here)))
        else:
            own.append(tuple(b - h for b, h in zip(before, here)))
        before = here
    for span in range(spans):
        first = second = cross = None
        for lag in range(min(span + 1, len(taps))):
            (tr, ti), (xr, xi) = taps[lag], own[span - lag]
            if lag == 0:
                first, second, cross = tr * xr, ti * xi, tr * xi + ti * xr
            else:
                first, second = first + tr * xr, second + ti * xi
                cross = cross + tr * xi + ti * xr
        real, imag = first - second, cross
        if edge:
            at_edge = lax.broadcasted_iota(jnp.int32, real.shape, 0) == 0
            real, imag = jnp.where(at_edge, first, real), jnp.where(at_edge, second, imag)
        cols = slice((span % 2) * share, (span % 2 + 1) * share)
        total_ref[span // 2, real_rows, cols] = real
        total_ref[span // 2, imag_rows, cols] = imag


def fused_kernel(
    n, q_hbm, k_hbm, v_hbm, taps_hbm, skip_ref, w_hbm, fwd_hbm, inv_hbm, out_ref,
    q_ref, k_ref, v_ref, taps_ref, w_ref, fwd_ref, inv_ref,
    mixed, recv1, spec_b, spec_x, total, total_b, send2, recv2, gated, s1, r1, s2, r2, acc,
    load_sem, own1_sem, own2_sem, a_send, a_recv, b_send, b_recv, c_send, c_recv, d_send, d_recv,
):
    me, ch = lax.axis_index("ctx"), lax.axis_index("ch")
    y, core = ch // 2, ch % 2
    beside, across = y * 2 + 1 - core, (1 - y) * 2 + core
    opposite = (1 - y) * 2 + 1 - core
    length, width = q_hbm.shape
    share, depth = width // n, length // CHUNKS
    offsets = sorted(range(1, n), key=lambda o: abs(o - n // 2))

    def load(index, src, dst):
        copy = pltpu.make_async_copy(src, dst, load_sem.at[index])
        copy.start()
        return copy

    taps_cols = pl.ds(pl.multiple_of(me * share, share), share)
    load_k, load_v = load(0, k_hbm, k_ref), load(1, v_hbm, v_ref)
    load_fwd = load(2, fwd_hbm, fwd_ref)
    load_taps = load(3, taps_hbm.at[:, taps_cols], taps_ref)
    load_inv, load_q = load(4, inv_hbm, inv_ref), load(5, q_hbm, q_ref)
    load_w = [
        load(6 + i, w_hbm.at[:, pl.ds(pl.multiple_of(owner * width, width), width)], w_ref.at[i])
        for i, owner in enumerate((opposite, beside, across, ch))
    ]

    barrier = pltpu.get_barrier_semaphore()
    for o in offsets:
        peer = {"ctx": lax.rem(me + o, n)}
        pl.semaphore_signal(barrier, inc=1, device_id=peer, device_id_type=MESH)
    for other in (beside, across):
        pl.semaphore_signal(barrier, inc=1, device_id={"ch": other}, device_id_type=MESH)

    load_k.wait()
    load_v.wait()
    for d in range(n):
        cols = slice(d * share, (d + 1) * share)
        mixed[d] = (k_ref[:, cols].astype(F32) * v_ref[:, cols].astype(F32)).astype(BF16)
    pl.semaphore_wait(barrier, n + 1)

    def half(index):
        return pl.ds(pl.multiple_of(lax.rem(index, 2) * share, share), share)

    def span_copy(peer, src, landing, sem_out, sem_in):
        return pltpu.make_async_remote_copy(
            src_ref=mixed.at[src],
            dst_ref=recv1.at[landing // 2, :, half(landing)],
            send_sem=a_send.at[sem_out],
            recv_sem=a_recv.at[sem_in],
            device_id={"ctx": peer},
            device_id_type=MESH,
        )

    sends = []
    for o in offsets:
        peer = lax.rem(me + o, n)
        copy = span_copy(peer, peer, me, o - 1, me)
        copy.start()
        sends.append(copy)
    own = pltpu.make_async_copy(mixed.at[me], recv1.at[me // 2, :, half(me)], own1_sem)
    own.start()

    load_fwd.wait()
    load_taps.wait()
    for p in range(spec_b.shape[0]):
        blocks = [taps_ref[(2 * p + i) * length : (2 * p + i + 1) * length] for i in range(2)]
        spec_b[p] = jnp.dot(
            fwd_ref[...], jnp.concatenate(blocks, axis=1).astype(BF16), preferred_element_type=F32
        )
    own.wait()
    for p in range(n // 2):
        for src in (2 * p, 2 * p + 1):

            @pl.when(src != me)
            def _():
                cols = slice((src % 2) * share, (src % 2 + 1) * share)
                pltpu.make_async_remote_copy(
                    src_ref=mixed.at[src],
                    dst_ref=recv1.at[src // 2, :, cols],
                    send_sem=a_send.at[0],
                    recv_sem=a_recv.at[src],
                    device_id={"ctx": lax.rem(me + 1, n)},
                    device_id_type=MESH,
                ).wait_recv()

        spec_x[p] = jnp.dot(fwd_ref[...], recv1[p], preferred_element_type=F32)

    spectral_tile(0, 1, True, spec_b, spec_x, total)
    tiles = length // 2 // ROWS

    def even(i, carry):
        spectral_tile(pl.multiple_of(i * ROWS, ROWS), 1, False, spec_b, spec_x, total)
        return carry

    def odd(i, carry):
        spectral_tile(pl.multiple_of(i * ROWS, ROWS), -1, False, spec_b, spec_x, total)
        return carry

    lax.fori_loop(1, tiles, even, 0)
    lax.fori_loop(tiles, 2 * tiles, odd, 0)
    for p in range(n // 2):
        total_b[p] = total[p].astype(BF16)

    load_inv.wait()
    own_copies = []
    for t in range(CHUNKS):
        rows = slice(t * depth, (t + 1) * depth)
        for p in range(n // 2):
            conv = jnp.dot(inv_ref[rows], total_b[p], preferred_element_type=F32).astype(BF16)
            send2[t, 2 * p] = conv[:, :share]
            send2[t, 2 * p + 1] = conv[:, share:]
        for o in offsets:
            peer = lax.rem(me + o, n)
            copy = pltpu.make_async_remote_copy(
                src_ref=send2.at[t, peer],
                dst_ref=recv2.at[rows, taps_cols],
                send_sem=b_send.at[t, o - 1],
                recv_sem=b_recv.at[t, o - 1],
                device_id={"ctx": peer},
                device_id_type=MESH,
            )
            copy.start()
            sends.append(copy)
        copy = pltpu.make_async_copy(send2.at[t, me], recv2.at[rows, taps_cols], own2_sem.at[t])
        copy.start()
        own_copies.append(copy)

    def exchange(src, dst, out_sem, in_sem, other):
        copy = pltpu.make_async_remote_copy(
            src_ref=src,
            dst_ref=dst,
            send_sem=out_sem,
            recv_sem=in_sem,
            device_id={"ch": other},
            device_id_type=MESH,
        )
        copy.start()
        sends.append(copy)
        return copy

    def project(block):
        return jnp.dot(gated[...], w_ref[block], preferred_element_type=F32)

    def finish(t, copy):
        copy.wait_recv()
        rows = slice(t * depth, (t + 1) * depth)
        out_ref[rows] = (acc[t] + r2[t].astype(F32)).astype(BF16)

    load_q.wait()
    for copy in load_w:
        copy.wait()
    last = None
    for t in range(CHUNKS):
        rows = slice(t * depth, (t + 1) * depth)
        own_copies[t].wait()
        for o in offsets:
            src = lax.rem(me + n - o, n)
            pltpu.make_async_remote_copy(
                src_ref=send2.at[t, src],
                dst_ref=recv2.at[rows, pl.ds(pl.multiple_of(src * share, share), share)],
                send_sem=b_send.at[t, o - 1],
                recv_sem=b_recv.at[t, o - 1],
                device_id={"ctx": src},
                device_id_type=MESH,
            ).wait_recv()
        for d in range(n):
            cols = slice(d * share, (d + 1) * share)
            conv = recv2[rows, cols].astype(F32)
            conv = conv + skip_ref[:, cols] * mixed[d, rows].astype(F32)
            gated[:, cols] = (q_ref[rows, cols].astype(F32) * conv).astype(BF16)
        s1[t, 0] = project(0).astype(BF16)
        far = exchange(s1.at[t, 0], r1.at[t, 0], c_send.at[t, 0], c_recv.at[t, 0], beside)
        s1[t, 1] = project(1).astype(BF16)
        near = exchange(s1.at[t, 1], r1.at[t, 1], c_send.at[t, 1], c_recv.at[t, 1], beside)
        passed = project(2)
        far.wait_recv()
        s2[t] = (passed + r1[t, 0].astype(F32)).astype(BF16)
        final = exchange(s2.at[t], r2.at[t], d_send.at[t], d_recv.at[t], across)
        kept = project(3)
        near.wait_recv()
        acc[t] = kept + r1[t, 1].astype(F32)
        if last is not None:
            finish(t - 1, last)
        last = final
    finish(CHUNKS - 1, last)
    for copy in sends:
        copy.wait_send()


def fused_body(forward, inverse, query_gate, key_gate, value_in, filter_taps, skip_gain, out_weight):
    length, width = query_gate.shape
    n = lax.axis_size("ctx")
    share, depth, taps = width // n, length // CHUNKS, filter_taps.shape[0]
    dma = pltpu.SemaphoreType.DMA
    anywhere = pl.BlockSpec(memory_space=pl.ANY)
    vmem = pl.BlockSpec(memory_space=pltpu.VMEM)
    return pl.pallas_call(
        functools.partial(fused_kernel, n),
        out_shape=jax.ShapeDtypeStruct((length, width), BF16),
        in_specs=[anywhere] * 4 + [vmem] + [anywhere] * 3,
        out_specs=vmem,
        scratch_shapes=[
            pltpu.VMEM((length, width), BF16),
            pltpu.VMEM((length, width), BF16),
            pltpu.VMEM((length, width), BF16),
            pltpu.VMEM((taps, share), F32),
            pltpu.VMEM((4, width, width), BF16),
            pltpu.VMEM((2 * length, length), BF16),
            pltpu.VMEM((length, 2 * length), BF16),
            pltpu.VMEM((n, length, share), BF16),
            pltpu.VMEM((n // 2, length, 2 * share), BF16),
            pltpu.VMEM((taps // length // 2, 2 * length, 2 * share), F32),
            pltpu.VMEM((n // 2, 2 * length, 2 * share), F32),
            pltpu.VMEM((n // 2, 2 * length, 2 * share), F32),
            pltpu.VMEM((n // 2, 2 * length, 2 * share), BF16),
            pltpu.VMEM((CHUNKS, n, depth, share), BF16),
            pltpu.VMEM((length, width), BF16),
            pltpu.VMEM((depth, width), BF16),
            pltpu.VMEM((CHUNKS, 2, depth, width), BF16),
            pltpu.VMEM((CHUNKS, 2, depth, width), BF16),
            pltpu.VMEM((CHUNKS, depth, width), BF16),
            pltpu.VMEM((CHUNKS, depth, width), BF16),
            pltpu.VMEM((CHUNKS, depth, width), F32),
            dma((10,)),
            dma,
            dma((CHUNKS,)),
            dma((n - 1,)),
            dma((n,)),
            dma((CHUNKS, n - 1)),
            dma((CHUNKS, n - 1)),
            dma((CHUNKS, 2)),
            dma((CHUNKS, 2)),
            dma((CHUNKS,)),
            dma((CHUNKS,)),
        ],
        compiler_params=pltpu.CompilerParams(
            collective_id=0, has_side_effects=True, vmem_limit_bytes=56 * 2**20
        ),
        cost_estimate=pl.CostEstimate(
            flops=10 * 10**9, bytes_accessed=16 * 2**20, transcendentals=0
        ),
    )(
        query_gate, key_gate, value_in, filter_taps, skip_gain.reshape(1, width), out_weight,
        forward, inverse,
    )


def solution(mesh):
    in_specs = (
        P("ctx", "ch"),
        P("ctx", "ch"),
        P("ctx", "ch"),
        P(None, "ch"),
        P("ch"),
        P("ch", None),
    )
    out_specs = P("ctx", "ch")

    def whole(query_gate, *rest):
        length = query_gate.shape[0] // mesh.shape["ctx"]
        width = query_gate.shape[1] // mesh.shape["ch"]
        forward, inverse = transform_tables(length)
        taps = rest[2].shape[0] // length
        fits = mesh.shape["ch"] == 4 and width == 128 * mesh.shape["ctx"]
        fits = fits and mesh.shape["ctx"] % 2 == 0 and taps % 2 == 0 and length % 128 == 0
        chosen = fused_body if fits else plain_body

        def body(*args):
            return chosen(jnp.asarray(forward), jnp.asarray(inverse), *args)

        return jax.shard_map(
            body, mesh=mesh, in_specs=in_specs, out_specs=out_specs, check_vma=False
        )(query_gate, *rest)

    return whole
```

```python
import functools

import ml_dtypes
import numpy as np

import jax
import jax.numpy as jnp
from jax import lax
from jax.experimental import pallas as pl
from jax.experimental.pallas import tpu as pltpu
from jax.sharding import PartitionSpec as P

BF16 = jnp.bfloat16
F32 = jnp.float32


def transform_tables(length):
    freqs = np.concatenate([np.arange(0, length, 2), np.arange(1, length, 2)])[:, None]
    times = np.arange(length)[None, :]
    angle = (freqs * times % (2 * length)) * (np.pi / length)
    real, imag = np.cos(angle), -np.sin(angle)
    imag[0] = 1.0 - 2.0 * (np.arange(length) % 2)
    forward = np.concatenate([real, imag], axis=0)
    angle = (freqs * (times + length) % (2 * length)) * (np.pi / length)
    real, imag = np.cos(angle) / length, -np.sin(angle) / length
    real[0] = 0.5 / length
    imag[0] = (1.0 - 2.0 * ((np.arange(length) + length) % 2)) * 0.5 / length
    inverse = np.concatenate([real, imag], axis=0).T
    return forward.astype(ml_dtypes.bfloat16), inverse.astype(ml_dtypes.bfloat16)


def long_conv(x, taps, forward, inverse):
    spans, length, _ = x.shape
    win = taps.shape[0]
    data = jnp.einsum("mn,knc->kmc", forward, x, preferred_element_type=F32)
    block = jnp.einsum("mn,knc->kmc", forward, taps, preferred_element_type=F32)
    parity = jnp.where(jnp.arange(2 * length) % length < length // 2, 1.0, -1.0)[None, :, None]
    before = jnp.concatenate([jnp.zeros_like(data[:1]), data[:-1]], axis=0)
    pair = before + parity * data
    edge = (jnp.arange(length) == 0)[None, :, None]
    real = jnp.zeros_like(data[:, :length])
    imag = jnp.zeros_like(real)
    for lag in range(min(win, spans)):
        own = jnp.concatenate([jnp.zeros_like(pair[:lag]), pair[: spans - lag]], axis=0)
        own_real, own_imag = own[:, :length], own[:, length:]
        tap_real, tap_imag = block[lag, :length][None], block[lag, length:][None]
        first, second = tap_real * own_real, tap_imag * own_imag
        real = real + jnp.where(edge, first, first - second)
        imag = imag + jnp.where(edge, second, tap_real * own_imag + tap_imag * own_real)
    total = jnp.concatenate([real, imag], axis=1).astype(BF16)
    return jnp.einsum("im,kmc->kic", inverse, total, preferred_element_type=F32)


def plain_body(forward, inverse, query_gate, key_gate, value_in, filter_taps, skip_gain, out_weight):
    length, width = query_gate.shape
    devices = lax.axis_size("ctx")
    share = width // devices
    mixed_in = (key_gate.astype(F32) * value_in.astype(F32)).astype(BF16)
    x = lax.all_to_all(mixed_in, "ctx", split_axis=1, concat_axis=0, tiled=True)
    taps = lax.dynamic_slice_in_dim(filter_taps, lax.axis_index("ctx") * share, share, axis=1)
    conv = long_conv(
        x.reshape(devices, length, share),
        taps.astype(BF16).reshape(-1, length, share),
        forward,
        inverse,
    )
    conv = conv.astype(BF16).reshape(devices * length, share)
    conv = lax.all_to_all(conv, "ctx", split_axis=0, concat_axis=1, tiled=True)
    combined = conv.astype(F32) + skip_gain[None, :] * mixed_in.astype(F32)
    gated = (query_gate.astype(F32) * combined).astype(BF16)
    partial_value = jnp.dot(gated, out_weight, preferred_element_type=F32)
    return lax.psum_scatter(partial_value.astype(BF16), "ch", scatter_dimension=1, tiled=True)


MESH = pl.DeviceIdType.MESH
EIGHTHS = (2, 2, 2, 1, 1)
ROWS = 8


def spectral_tile(row, sign, edge, outs, ins, add, taps_ref, data_ref, total_ref):
    pairs, height, lanes = data_ref.shape
    share, lags = lanes // 2, 2 * taps_ref.shape[0]
    real_rows, imag_rows = pl.ds(row, ROWS), pl.ds(row + height // 2, ROWS)

    def parts(ref, index):
        cols = slice((index % 2) * share, (index % 2 + 1) * share)
        return ref[index // 2, real_rows, cols], ref[index // 2, imag_rows, cols]

    used = sorted({o - i for o in outs for i in ins if 0 <= o - i < lags})
    taps = {lag: parts(taps_ref, lag) for lag in used}
    own = {}
    before = parts(data_ref, ins[0] - 1) if ins[0] > 0 else None
    for span in ins:
        here = parts(data_ref, span)
        if before is None:
            own[span] = here if sign > 0 else tuple(-part for part in here)
        elif sign > 0:
            own[span] = tuple(b + h for b, h in zip(before, here))
        else:
            own[span] = tuple(b - h for b, h in zip(before, here))
        before = here
    for out in outs:
        first = second = cross = None
        for span in ins:
            if not 0 <= out - span < lags:
                continue
            (tr, ti), (xr, xi) = taps[out - span], own[span]
            if first is None:
                first, second, cross = tr * xr, ti * xi, tr * xi + ti * xr
            else:
                first, second = first + tr * xr, second + ti * xi
                cross = cross + tr * xi + ti * xr
        cols = slice((out % 2) * share, (out % 2 + 1) * share)
        if first is None:
            if not add:
                total_ref[out // 2, real_rows, cols] = jnp.zeros((ROWS, share), F32)
                total_ref[out // 2, imag_rows, cols] = jnp.zeros((ROWS, share), F32)
            continue
        real, imag = first - second, cross
        if edge:
            at_edge = lax.broadcasted_iota(jnp.int32, real.shape, 0) == 0
            real, imag = jnp.where(at_edge, first, real), jnp.where(at_edge, second, imag)
        if add:
            real += total_ref[out // 2, real_rows, cols]
            imag += total_ref[out // 2, imag_rows, cols]
        total_ref[out // 2, real_rows, cols] = real
        total_ref[out // 2, imag_rows, cols] = imag


def spectral_sums(outs, ins, add, taps_ref, data_ref, total_ref):
    refs = (taps_ref, data_ref, total_ref)
    tiles = data_ref.shape[1] // 4 // ROWS
    spectral_tile(0, 1, True, outs, ins, add, *refs)

    def even(i, carry):
        spectral_tile(pl.multiple_of(i * ROWS, ROWS), 1, False, outs, ins, add, *refs)
        return carry

    def odd(i, carry):
        spectral_tile(pl.multiple_of(i * ROWS, ROWS), -1, False, outs, ins, add, *refs)
        return carry

    lax.fori_loop(1, tiles, even, 0)
    lax.fori_loop(tiles, 2 * tiles, odd, 0)


def chunk_rows(length):
    ends = np.cumsum((0,) + EIGHTHS) * (length // 8)
    return [slice(int(a), int(b)) for a, b in zip(ends[:-1], ends[1:])]


def fused_kernel(
    n, q_hbm, k_hbm, v_hbm, taps_hbm, skip_ref, w_hbm, fwd_hbm, inv_hbm, out_ref,
    q_ref, k_ref, v_ref, taps_ref, w_ref, fwd_ref, inv_ref,
    mixed, recv1, spec_b, spec_x, total, total_b, send2, recv2, gated, s1, r1, s2, r2, acc,
    load_sem, own1_sem, own2_sem, a_send, a_recv, b_send, b_recv, c_send, c_recv, d_send, d_recv,
):
    me, ch = lax.axis_index("ctx"), lax.axis_index("ch")
    y, core = ch // 2, ch % 2
    beside, across = y * 2 + 1 - core, (1 - y) * 2 + core
    opposite = (1 - y) * 2 + 1 - core
    length, width = q_hbm.shape
    share, group = width // n, n // 2
    chunks = chunk_rows(length)
    side = me // group
    here = [side * group + lax.rem(me + i, group) for i in range(group)]
    there = [(1 - side) * group + lax.rem(me + i, group) for i in range(group)]
    order = [there[0]]
    for i in range(1, group):
        order += [here[i], there[i]]

    def load(index, src, dst):
        copy = pltpu.make_async_copy(src, dst, load_sem.at[index])
        copy.start()
        return copy

    taps_cols = pl.ds(pl.multiple_of(me * share, share), share)
    load_k, load_v = load(0, k_hbm, k_ref), load(1, v_hbm, v_ref)
    load_fwd = load(2, fwd_hbm, fwd_ref)
    load_taps = load(3, taps_hbm.at[:, taps_cols], taps_ref)
    load_inv, load_q = load(4, inv_hbm, inv_ref), load(5, q_hbm, q_ref)
    load_w = [
        load(6 + i, w_hbm.at[:, pl.ds(pl.multiple_of(owner * width, width), width)], w_ref.at[i])
        for i, owner in enumerate((opposite, beside, across, ch))
    ]

    barrier = pltpu.get_barrier_semaphore()
    for peer in order:
        pl.semaphore_signal(barrier, inc=1, device_id={"ctx": peer}, device_id_type=MESH)
    for other in (beside, across):
        pl.semaphore_signal(barrier, inc=1, device_id={"ch": other}, device_id_type=MESH)

    load_k.wait()
    load_v.wait()
    for d in range(n):
        cols = slice(d * share, (d + 1) * share)
        mixed[d] = (k_ref[:, cols].astype(F32) * v_ref[:, cols].astype(F32)).astype(BF16)
    pl.semaphore_wait(barrier, n + 1)

    def half(index):
        return pl.ds(pl.multiple_of(lax.rem(index, 2) * share, share), share)

    sends = []
    for i, peer in enumerate(order):
        copy = pltpu.make_async_remote_copy(
            src_ref=mixed.at[peer],
            dst_ref=recv1.at[me // 2, :, half(me)],
            send_sem=a_send.at[i],
            recv_sem=a_recv.at[me],
            device_id={"ctx": peer},
            device_id_type=MESH,
        )
        copy.start()
        sends.append(copy)
    own = pltpu.make_async_copy(mixed.at[me], recv1.at[me // 2, :, half(me)], own1_sem)
    own.start()

    load_fwd.wait()
    load_taps.wait()
    for p in range(spec_b.shape[0]):
        blocks = [taps_ref[(2 * p + i) * length : (2 * p + i + 1) * length] for i in range(2)]
        spec_b[p] = jnp.dot(
            fwd_ref[...], jnp.concatenate(blocks, axis=1).astype(BF16), preferred_element_type=F32
        )
    own.wait()

    def spectrum(p):
        for src in (2 * p, 2 * p + 1):

            @pl.when(src != me)
            def _():
                cols = slice((src % 2) * share, (src % 2 + 1) * share)
                pltpu.make_async_remote_copy(
                    src_ref=mixed.at[src],
                    dst_ref=recv1.at[src // 2, :, cols],
                    send_sem=a_send.at[0],
                    recv_sem=a_recv.at[src],
                    device_id={"ctx": order[0]},
                    device_id_type=MESH,
                ).wait_recv()

        spec_x[p] = jnp.dot(fwd_ref[...], recv1[p], preferred_element_type=F32)

    def way_back(t, peer):
        return pltpu.make_async_remote_copy(
            src_ref=send2.at[peer, chunks[t]],
            dst_ref=recv2.at[chunks[t], taps_cols],
            send_sem=b_send.at[t, peer],
            recv_sem=b_recv.at[t, me],
            device_id={"ctx": peer},
            device_id_type=MESH,
        )

    def own_rows(t):
        return pltpu.make_async_copy(
            send2.at[me, chunks[t]], recv2.at[chunks[t], taps_cols], own2_sem.at[t]
        )

    def send_back(which):
        pairs = range(which * group // 2, (which + 1) * group // 2)
        for p in pairs:
            total_b[p] = total[p].astype(BF16)
        for t, rows in enumerate(chunks):
            for p in pairs:
                conv = jnp.dot(inv_ref[rows], total_b[p], preferred_element_type=F32).astype(BF16)
                send2[2 * p, rows] = conv[:, :share]
                send2[2 * p + 1, rows] = conv[:, share:]

            @pl.when(side == which)
            def _():
                own_rows(t).start()

            @pl.when(side != which)
            def _():
                way_back(t, which * group + lax.rem(me, group)).start()

            for i in range(1, group):
                way_back(t, which * group + lax.rem(me + i, group)).start()

    low, high = range(group), range(group, n)
    for p in range(group // 2):
        spectrum(p)
    spectral_sums(low, low, False, spec_b, spec_x, total)
    load_inv.wait()
    send_back(0)
    spectral_sums(high, low, False, spec_b, spec_x, total)
    for p in range(group // 2, group):
        spectrum(p)
    spectral_sums(high, high, True, spec_b, spec_x, total)
    send_back(1)

    def exchange(src, dst, out_sem, in_sem, other):
        copy = pltpu.make_async_remote_copy(
            src_ref=src,
            dst_ref=dst,
            send_sem=out_sem,
            recv_sem=in_sem,
            device_id={"ch": other},
            device_id_type=MESH,
        )
        copy.start()
        sends.append(copy)
        return copy

    def project(rows, block):
        return jnp.dot(gated[rows], w_ref[block], preferred_element_type=F32)

    def finish(t, copy):
        copy.wait_recv()
        out_ref[chunks[t]] = (acc[chunks[t]] + r2[chunks[t]].astype(F32)).astype(BF16)

    load_q.wait()
    for copy in load_w:
        copy.wait()
    last = None
    for t, rows in enumerate(chunks):
        own_rows(t).wait()
        for src in range(n):

            @pl.when(src != me)
            def _():
                cols = slice(src * share, (src + 1) * share)
                pltpu.make_async_remote_copy(
                    src_ref=send2.at[src, rows],
                    dst_ref=recv2.at[rows, cols],
                    send_sem=b_send.at[t, src],
                    recv_sem=b_recv.at[t, src],
                    device_id={"ctx": order[0]},
                    device_id_type=MESH,
                ).wait_recv()

        for d in range(n):
            cols = slice(d * share, (d + 1) * share)
            conv = recv2[rows, cols].astype(F32)
            conv = conv + skip_ref[:, cols] * mixed[d, rows].astype(F32)
            gated[rows, cols] = (q_ref[rows, cols].astype(F32) * conv).astype(BF16)
        s1[0, rows] = project(rows, 0).astype(BF16)
        far = exchange(s1.at[0, rows], r1.at[0, rows], c_send.at[t, 0], c_recv.at[t, 0], beside)
        passed = project(rows, 2)
        far.wait_recv()
        s2[rows] = (passed + r1[0, rows].astype(F32)).astype(BF16)
        final = exchange(s2.at[rows], r2.at[rows], d_send.at[t], d_recv.at[t], across)
        s1[1, rows] = project(rows, 1).astype(BF16)
        near = exchange(s1.at[1, rows], r1.at[1, rows], c_send.at[t, 1], c_recv.at[t, 1], beside)
        kept = project(rows, 3)
        near.wait_recv()
        acc[rows] = kept + r1[1, rows].astype(F32)
        if last is not None:
            finish(t - 1, last)
        last = final
    finish(len(chunks) - 1, last)
    for copy in sends:
        copy.wait_send()
    for t in range(len(chunks)):
        for i in range(1, group):
            way_back(t, here[i]).wait_send()
        for peer in there:
            way_back(t, peer).wait_send()


def fused_body(forward, inverse, query_gate, key_gate, value_in, filter_taps, skip_gain, out_weight):
    length, width = query_gate.shape
    n = lax.axis_size("ctx")
    share, taps, chunks = width // n, filter_taps.shape[0], len(EIGHTHS)
    dma = pltpu.SemaphoreType.DMA
    anywhere = pl.BlockSpec(memory_space=pl.ANY)
    vmem = pl.BlockSpec(memory_space=pltpu.VMEM)
    return pl.pallas_call(
        functools.partial(fused_kernel, n),
        out_shape=jax.ShapeDtypeStruct((length, width), BF16),
        in_specs=[anywhere] * 4 + [vmem] + [anywhere] * 3,
        out_specs=vmem,
        scratch_shapes=[
            pltpu.VMEM((length, width), BF16),
            pltpu.VMEM((length, width), BF16),
            pltpu.VMEM((length, width), BF16),
            pltpu.VMEM((taps, share), F32),
            pltpu.VMEM((4, width, width), BF16),
            pltpu.VMEM((2 * length, length), BF16),
            pltpu.VMEM((length, 2 * length), BF16),
            pltpu.VMEM((n, length, share), BF16),
            pltpu.VMEM((n // 2, length, 2 * share), BF16),
            pltpu.VMEM((taps // length // 2, 2 * length, 2 * share), F32),
            pltpu.VMEM((n // 2, 2 * length, 2 * share), F32),
            pltpu.VMEM((n // 2, 2 * length, 2 * share), F32),
            pltpu.VMEM((n // 2, 2 * length, 2 * share), BF16),
            pltpu.VMEM((n, length, share), BF16),
            pltpu.VMEM((length, width), BF16),
            pltpu.VMEM((length, width), BF16),
            pltpu.VMEM((2, length, width), BF16),
            pltpu.VMEM((2, length, width), BF16),
            pltpu.VMEM((length, width), BF16),
            pltpu.VMEM((length, width), BF16),
            pltpu.VMEM((length, width), F32),
            dma((10,)),
            dma,
            dma((chunks,)),
            dma((n - 1,)),
            dma((n,)),
            dma((chunks, n)),
            dma((chunks, n)),
            dma((chunks, 2)),
            dma((chunks, 2)),
            dma((chunks,)),
            dma((chunks,)),
        ],
        compiler_params=pltpu.CompilerParams(
            collective_id=0, has_side_effects=True, vmem_limit_bytes=56 * 2**20
        ),
        cost_estimate=pl.CostEstimate(
            flops=10 * 10**9, bytes_accessed=16 * 2**20, transcendentals=0
        ),
    )(
        query_gate, key_gate, value_in, filter_taps, skip_gain.reshape(1, width), out_weight,
        forward, inverse,
    )


def solution(mesh):
    in_specs = (
        P("ctx", "ch"),
        P("ctx", "ch"),
        P("ctx", "ch"),
        P(None, "ch"),
        P("ch"),
        P("ch", None),
    )
    out_specs = P("ctx", "ch")

    def whole(query_gate, *rest):
        length = query_gate.shape[0] // mesh.shape["ctx"]
        width = query_gate.shape[1] // mesh.shape["ch"]
        forward, inverse = transform_tables(length)
        taps = rest[2].shape[0] // length
        fits = mesh.shape["ch"] == 4 and width == 128 * mesh.shape["ctx"]
        fits = fits and mesh.shape["ctx"] % 4 == 0 and taps % 2 == 0 and length % 128 == 0
        chosen = fused_body if fits else plain_body

        def body(*args):
            return chosen(jnp.asarray(forward), jnp.asarray(inverse), *args)

        return jax.shard_map(
            body, mesh=mesh, in_specs=in_specs, out_specs=out_specs, check_vma=False
        )(query_gate, *rest)

    return whole
```

```python
import functools

import ml_dtypes
import numpy as np

import jax
import jax.numpy as jnp
from jax import lax
from jax.experimental import pallas as pl
from jax.experimental.pallas import tpu as pltpu
from jax.sharding import PartitionSpec as P

BF16 = jnp.bfloat16
F32 = jnp.float32


def transform_tables(length):
    freqs = np.concatenate([np.arange(0, length, 2), np.arange(1, length, 2)])[:, None]
    times = np.arange(length)[None, :]
    angle = (freqs * times % (2 * length)) * (np.pi / length)
    real, imag = np.cos(angle), -np.sin(angle)
    imag[0] = 1.0 - 2.0 * (np.arange(length) % 2)
    forward = np.concatenate([real, imag], axis=0)
    angle = (freqs * (times + length) % (2 * length)) * (np.pi / length)
    real, imag = np.cos(angle) / length, -np.sin(angle) / length
    real[0] = 0.5 / length
    imag[0] = (1.0 - 2.0 * ((np.arange(length) + length) % 2)) * 0.5 / length
    inverse = np.concatenate([real, imag], axis=0).T
    return forward.astype(ml_dtypes.bfloat16), inverse.astype(ml_dtypes.bfloat16)


def long_conv(x, taps, forward, inverse):
    spans, length, _ = x.shape
    win = taps.shape[0]
    data = jnp.einsum("mn,knc->kmc", forward, x, preferred_element_type=F32)
    block = jnp.einsum("mn,knc->kmc", forward, taps, preferred_element_type=F32)
    parity = jnp.where(jnp.arange(2 * length) % length < length // 2, 1.0, -1.0)[None, :, None]
    before = jnp.concatenate([jnp.zeros_like(data[:1]), data[:-1]], axis=0)
    pair = before + parity * data
    edge = (jnp.arange(length) == 0)[None, :, None]
    real = jnp.zeros_like(data[:, :length])
    imag = jnp.zeros_like(real)
    for lag in range(min(win, spans)):
        own = jnp.concatenate([jnp.zeros_like(pair[:lag]), pair[: spans - lag]], axis=0)
        own_real, own_imag = own[:, :length], own[:, length:]
        tap_real, tap_imag = block[lag, :length][None], block[lag, length:][None]
        first, second = tap_real * own_real, tap_imag * own_imag
        real = real + jnp.where(edge, first, first - second)
        imag = imag + jnp.where(edge, second, tap_real * own_imag + tap_imag * own_real)
    total = jnp.concatenate([real, imag], axis=1).astype(BF16)
    return jnp.einsum("im,kmc->kic", inverse, total, preferred_element_type=F32)


def plain_body(forward, inverse, query_gate, key_gate, value_in, filter_taps, skip_gain, out_weight):
    length, width = query_gate.shape
    devices = lax.axis_size("ctx")
    share = width // devices
    mixed_in = (key_gate.astype(F32) * value_in.astype(F32)).astype(BF16)
    x = lax.all_to_all(mixed_in, "ctx", split_axis=1, concat_axis=0, tiled=True)
    taps = lax.dynamic_slice_in_dim(filter_taps, lax.axis_index("ctx") * share, share, axis=1)
    conv = long_conv(
        x.reshape(devices, length, share),
        taps.astype(BF16).reshape(-1, length, share),
        forward,
        inverse,
    )
    conv = conv.astype(BF16).reshape(devices * length, share)
    conv = lax.all_to_all(conv, "ctx", split_axis=0, concat_axis=1, tiled=True)
    combined = conv.astype(F32) + skip_gain[None, :] * mixed_in.astype(F32)
    gated = (query_gate.astype(F32) * combined).astype(BF16)
    partial_value = jnp.dot(gated, out_weight, preferred_element_type=F32)
    return lax.psum_scatter(partial_value.astype(BF16), "ch", scatter_dimension=1, tiled=True)


MESH = pl.DeviceIdType.MESH
EIGHTHS = (2, 2, 2, 2)
ROWS = 8


def spectral_tile(row, sign, edge, outs, ins, add, taps_ref, data_ref, total_ref):
    pairs, height, lanes = data_ref.shape
    share, lags = lanes // 2, 2 * taps_ref.shape[0]
    real_rows, imag_rows = pl.ds(row, ROWS), pl.ds(row + height // 2, ROWS)

    def parts(ref, index):
        cols = slice((index % 2) * share, (index % 2 + 1) * share)
        return ref[index // 2, real_rows, cols], ref[index // 2, imag_rows, cols]

    used = sorted({o - i for o in outs for i in ins if 0 <= o - i < lags})
    taps = {lag: parts(taps_ref, lag) for lag in used}
    own = {}
    before = parts(data_ref, ins[0] - 1) if ins[0] > 0 else None
    for span in ins:
        here = parts(data_ref, span)
        if before is None:
            own[span] = here if sign > 0 else tuple(-part for part in here)
        elif sign > 0:
            own[span] = tuple(b + h for b, h in zip(before, here))
        else:
            own[span] = tuple(b - h for b, h in zip(before, here))
        before = here
    for out in outs:
        first = second = cross = None
        for span in ins:
            if not 0 <= out - span < lags:
                continue
            (tr, ti), (xr, xi) = taps[out - span], own[span]
            if first is None:
                first, second, cross = tr * xr, ti * xi, tr * xi + ti * xr
            else:
                first, second = first + tr * xr, second + ti * xi
                cross = cross + tr * xi + ti * xr
        cols = slice((out % 2) * share, (out % 2 + 1) * share)
        if first is None:
            if not add:
                total_ref[out // 2, real_rows, cols] = jnp.zeros((ROWS, share), F32)
                total_ref[out // 2, imag_rows, cols] = jnp.zeros((ROWS, share), F32)
            continue
        real, imag = first - second, cross
        if edge:
            at_edge = lax.broadcasted_iota(jnp.int32, real.shape, 0) == 0
            real, imag = jnp.where(at_edge, first, real), jnp.where(at_edge, second, imag)
        if add:
            real += total_ref[out // 2, real_rows, cols]
            imag += total_ref[out // 2, imag_rows, cols]
        total_ref[out // 2, real_rows, cols] = real
        total_ref[out // 2, imag_rows, cols] = imag


def spectral_sums(outs, ins, add, taps_ref, data_ref, total_ref):
    refs = (taps_ref, data_ref, total_ref)
    tiles = data_ref.shape[1] // 4 // ROWS
    spectral_tile(0, 1, True, outs, ins, add, *refs)

    def even(i, carry):
        spectral_tile(pl.multiple_of(i * ROWS, ROWS), 1, False, outs, ins, add, *refs)
        return carry

    def odd(i, carry):
        spectral_tile(pl.multiple_of(i * ROWS, ROWS), -1, False, outs, ins, add, *refs)
        return carry

    lax.fori_loop(1, tiles, even, 0)
    lax.fori_loop(tiles, 2 * tiles, odd, 0)


def chunk_rows(length):
    ends = np.cumsum((0,) + EIGHTHS) * (length // 8)
    return [slice(int(a), int(b)) for a, b in zip(ends[:-1], ends[1:])]


def fused_kernel(
    n, q_hbm, k_hbm, v_hbm, taps_hbm, skip_ref, w_hbm, fwd_hbm, inv_hbm, out_ref,
    q_ref, k_ref, v_ref, taps_ref, w_ref, fwd_ref, inv_ref,
    mixed, recv1, spec_b, spec_x, total, total_b, send2, recv2, gated, s1, r1, s2, r2, acc,
    load_sem, own1_sem, own2_sem, a_send, a_recv, b_send, b_recv, c_send, c_recv, d_send, d_recv,
):
    me, ch = lax.axis_index("ctx"), lax.axis_index("ch")
    y, core = ch // 2, ch % 2
    beside, across = y * 2 + 1 - core, (1 - y) * 2 + core
    opposite = (1 - y) * 2 + 1 - core
    length, width = q_hbm.shape
    share, group = width // n, n // 2
    chunks = chunk_rows(length)
    side = me // group
    here = [side * group + lax.rem(me + i, group) for i in range(group)]
    there = [(1 - side) * group + lax.rem(me + i, group) for i in range(group)]
    order = [there[0]]
    for i in range(1, group):
        order += [here[i], there[i]]

    def load(index, src, dst):
        copy = pltpu.make_async_copy(src, dst, load_sem.at[index])
        copy.start()
        return copy

    taps_cols = pl.ds(pl.multiple_of(me * share, share), share)
    load_k, load_v = load(0, k_hbm, k_ref), load(1, v_hbm, v_ref)
    load_fwd = load(2, fwd_hbm, fwd_ref)
    load_taps = load(3, taps_hbm.at[:, taps_cols], taps_ref)
    load_inv, load_q = load(4, inv_hbm, inv_ref), load(5, q_hbm, q_ref)
    load_w = [
        load(6 + i, w_hbm.at[:, pl.ds(pl.multiple_of(owner * width, width), width)], w_ref.at[i])
        for i, owner in enumerate((opposite, beside, across, ch))
    ]

    barrier = pltpu.get_barrier_semaphore()
    for peer in order:
        pl.semaphore_signal(barrier, inc=1, device_id={"ctx": peer}, device_id_type=MESH)
    for other in (beside, across):
        pl.semaphore_signal(barrier, inc=1, device_id={"ch": other}, device_id_type=MESH)

    load_k.wait()
    load_v.wait()
    for d in range(n):
        cols = slice(d * share, (d + 1) * share)
        mixed[d] = (k_ref[:, cols].astype(F32) * v_ref[:, cols].astype(F32)).astype(BF16)
    pl.semaphore_wait(barrier, n + 1)

    def half(index):
        return pl.ds(pl.multiple_of(lax.rem(index, 2) * share, share), share)

    sends = []
    for i, peer in enumerate(order):
        copy = pltpu.make_async_remote_copy(
            src_ref=mixed.at[peer],
            dst_ref=recv1.at[me // 2, :, half(me)],
            send_sem=a_send.at[i],
            recv_sem=a_recv.at[me],
            device_id={"ctx": peer},
            device_id_type=MESH,
        )
        copy.start()
        sends.append(copy)
    own = pltpu.make_async_copy(mixed.at[me], recv1.at[me // 2, :, half(me)], own1_sem)
    own.start()

    load_fwd.wait()
    load_taps.wait()
    for p in range(spec_b.shape[0]):
        blocks = [taps_ref[(2 * p + i) * length : (2 * p + i + 1) * length] for i in range(2)]
        spec_b[p] = jnp.dot(
            fwd_ref[...], jnp.concatenate(blocks, axis=1).astype(BF16), preferred_element_type=F32
        )
    own.wait()

    def spectrum(p):
        for src in (2 * p, 2 * p + 1):

            @pl.when(src != me)
            def _():
                cols = slice((src % 2) * share, (src % 2 + 1) * share)
                pltpu.make_async_remote_copy(
                    src_ref=mixed.at[src],
                    dst_ref=recv1.at[src // 2, :, cols],
                    send_sem=a_send.at[0],
                    recv_sem=a_recv.at[src],
                    device_id={"ctx": order[0]},
                    device_id_type=MESH,
                ).wait_recv()

        spec_x[p] = jnp.dot(fwd_ref[...], recv1[p], preferred_element_type=F32)

    def way_back(t, peer):
        return pltpu.make_async_remote_copy(
            src_ref=send2.at[peer, chunks[t]],
            dst_ref=recv2.at[chunks[t], taps_cols],
            send_sem=b_send.at[t, peer],
            recv_sem=b_recv.at[t, me],
            device_id={"ctx": peer},
            device_id_type=MESH,
        )

    def own_rows(t):
        return pltpu.make_async_copy(
            send2.at[me, chunks[t]], recv2.at[chunks[t], taps_cols], own2_sem.at[t]
        )

    def send_back(which):
        pairs = range(which * group // 2, (which + 1) * group // 2)
        for p in pairs:
            total_b[p] = total[p].astype(BF16)
        for t, rows in enumerate(chunks):
            for p in pairs:
                conv = jnp.dot(inv_ref[rows], total_b[p], preferred_element_type=F32).astype(BF16)
                send2[2 * p, rows] = conv[:, :share]
                send2[2 * p + 1, rows] = conv[:, share:]

            @pl.when(side == which)
            def _():
                own_rows(t).start()

            @pl.when(side != which)
            def _():
                way_back(t, which * group + lax.rem(me, group)).start()

            for i in range(1, group):
                way_back(t, which * group + lax.rem(me + i, group)).start()

    low, high = range(group), range(group, n)
    for p in range(group // 2):
        spectrum(p)
    spectral_sums(low, low, False, spec_b, spec_x, total)
    load_inv.wait()
    send_back(0)
    spectral_sums(high, low, False, spec_b, spec_x, total)
    for p in range(group // 2, group):
        spectrum(p)
    spectral_sums(high, high, True, spec_b, spec_x, total)
    send_back(1)

    def exchange(src, dst, out_sem, in_sem, other):
        copy = pltpu.make_async_remote_copy(
            src_ref=src,
            dst_ref=dst,
            send_sem=out_sem,
            recv_sem=in_sem,
            device_id={"ch": other},
            device_id_type=MESH,
        )
        copy.start()
        sends.append(copy)
        return copy

    def project(rows, block):
        return jnp.dot(gated[rows], w_ref[block], preferred_element_type=F32)

    def finish(t, copy):
        copy.wait_recv()
        out_ref[chunks[t]] = (acc[chunks[t]] + r2[chunks[t]].astype(F32)).astype(BF16)

    load_q.wait()
    for copy in load_w:
        copy.wait()
    last = None
    for t, rows in enumerate(chunks):
        own_rows(t).wait()
        for src in range(n):

            @pl.when(src != me)
            def _():
                cols = slice(src * share, (src + 1) * share)
                pltpu.make_async_remote_copy(
                    src_ref=send2.at[src, rows],
                    dst_ref=recv2.at[rows, cols],
                    send_sem=b_send.at[t, src],
                    recv_sem=b_recv.at[t, src],
                    device_id={"ctx": order[0]},
                    device_id_type=MESH,
                ).wait_recv()

        for d in range(n):
            cols = slice(d * share, (d + 1) * share)
            conv = recv2[rows, cols].astype(F32)
            conv = conv + skip_ref[:, cols] * mixed[d, rows].astype(F32)
            gated[rows, cols] = (q_ref[rows, cols].astype(F32) * conv).astype(BF16)
        s1[0, rows] = project(rows, 0).astype(BF16)
        far = exchange(s1.at[0, rows], r1.at[0, rows], c_send.at[t, 0], c_recv.at[t, 0], beside)
        s1[1, rows] = project(rows, 1).astype(BF16)
        near = exchange(s1.at[1, rows], r1.at[1, rows], c_send.at[t, 1], c_recv.at[t, 1], beside)
        passed = project(rows, 2)
        far.wait_recv()
        s2[rows] = (passed + r1[0, rows].astype(F32)).astype(BF16)
        final = exchange(s2.at[rows], r2.at[rows], d_send.at[t], d_recv.at[t], across)
        kept = project(rows, 3)
        near.wait_recv()
        acc[rows] = kept + r1[1, rows].astype(F32)
        if last is not None:
            finish(t - 1, last)
        last = final
    finish(len(chunks) - 1, last)
    for copy in sends:
        copy.wait_send()
    for t in range(len(chunks)):
        for i in range(1, group):
            way_back(t, here[i]).wait_send()
        for peer in there:
            way_back(t, peer).wait_send()


def fused_body(forward, inverse, query_gate, key_gate, value_in, filter_taps, skip_gain, out_weight):
    length, width = query_gate.shape
    n = lax.axis_size("ctx")
    share, taps, chunks = width // n, filter_taps.shape[0], len(EIGHTHS)
    dma = pltpu.SemaphoreType.DMA
    anywhere = pl.BlockSpec(memory_space=pl.ANY)
    vmem = pl.BlockSpec(memory_space=pltpu.VMEM)
    return pl.pallas_call(
        functools.partial(fused_kernel, n),
        out_shape=jax.ShapeDtypeStruct((length, width), BF16),
        in_specs=[anywhere] * 4 + [vmem] + [anywhere] * 3,
        out_specs=vmem,
        scratch_shapes=[
            pltpu.VMEM((length, width), BF16),
            pltpu.VMEM((length, width), BF16),
            pltpu.VMEM((length, width), BF16),
            pltpu.VMEM((taps, share), F32),
            pltpu.VMEM((4, width, width), BF16),
            pltpu.VMEM((2 * length, length), BF16),
            pltpu.VMEM((length, 2 * length), BF16),
            pltpu.VMEM((n, length, share), BF16),
            pltpu.VMEM((n // 2, length, 2 * share), BF16),
            pltpu.VMEM((taps // length // 2, 2 * length, 2 * share), F32),
            pltpu.VMEM((n // 2, 2 * length, 2 * share), F32),
            pltpu.VMEM((n // 2, 2 * length, 2 * share), F32),
            pltpu.VMEM((n // 2, 2 * length, 2 * share), BF16),
            pltpu.VMEM((n, length, share), BF16),
            pltpu.VMEM((length, width), BF16),
            pltpu.VMEM((length, width), BF16),
            pltpu.VMEM((2, length, width), BF16),
            pltpu.VMEM((2, length, width), BF16),
            pltpu.VMEM((length, width), BF16),
            pltpu.VMEM((length, width), BF16),
            pltpu.VMEM((length, width), F32),
            dma((10,)),
            dma,
            dma((chunks,)),
            dma((n - 1,)),
            dma((n,)),
            dma((chunks, n)),
            dma((chunks, n)),
            dma((chunks, 2)),
            dma((chunks, 2)),
            dma((chunks,)),
            dma((chunks,)),
        ],
        compiler_params=pltpu.CompilerParams(
            collective_id=0, has_side_effects=True, vmem_limit_bytes=56 * 2**20
        ),
        cost_estimate=pl.CostEstimate(
            flops=10 * 10**9, bytes_accessed=16 * 2**20, transcendentals=0
        ),
    )(
        query_gate, key_gate, value_in, filter_taps, skip_gain.reshape(1, width), out_weight,
        forward, inverse,
    )


def solution(mesh):
    in_specs = (
        P("ctx", "ch"),
        P("ctx", "ch"),
        P("ctx", "ch"),
        P(None, "ch"),
        P("ch"),
        P("ch", None),
    )
    out_specs = P("ctx", "ch")

    def whole(query_gate, *rest):
        length = query_gate.shape[0] // mesh.shape["ctx"]
        width = query_gate.shape[1] // mesh.shape["ch"]
        forward, inverse = transform_tables(length)
        taps = rest[2].shape[0] // length
        fits = mesh.shape["ch"] == 4 and width == 128 * mesh.shape["ctx"]
        fits = fits and mesh.shape["ctx"] % 4 == 0 and taps % 2 == 0 and length % 128 == 0
        chosen = fused_body if fits else plain_body

        def body(*args):
            return chosen(jnp.asarray(forward), jnp.asarray(inverse), *args)

        return jax.shard_map(
            body, mesh=mesh, in_specs=in_specs, out_specs=out_specs, check_vma=False
        )(query_gate, *rest)

    return whole
```

```python
import functools

import ml_dtypes
import numpy as np

import jax
import jax.numpy as jnp
from jax import lax
from jax.experimental import pallas as pl
from jax.experimental.pallas import tpu as pltpu
from jax.sharding import PartitionSpec as P

BF16 = jnp.bfloat16
F32 = jnp.float32


def transform_tables(length):
    freqs = np.concatenate([np.arange(0, length, 2), np.arange(1, length, 2)])[:, None]
    times = np.arange(length)[None, :]
    angle = (freqs * times % (2 * length)) * (np.pi / length)
    real, imag = np.cos(angle), -np.sin(angle)
    imag[0] = 1.0 - 2.0 * (np.arange(length) % 2)
    forward = np.concatenate([real, imag], axis=0)
    angle = (freqs * (times + length) % (2 * length)) * (np.pi / length)
    real, imag = np.cos(angle) / length, -np.sin(angle) / length
    real[0] = 0.5 / length
    imag[0] = (1.0 - 2.0 * ((np.arange(length) + length) % 2)) * 0.5 / length
    inverse = np.concatenate([real, imag], axis=0).T
    return forward.astype(ml_dtypes.bfloat16), inverse.astype(ml_dtypes.bfloat16)


def long_conv(x, taps, forward, inverse):
    spans, length, _ = x.shape
    win = taps.shape[0]
    data = jnp.einsum("mn,knc->kmc", forward, x, preferred_element_type=F32)
    block = jnp.einsum("mn,knc->kmc", forward, taps, preferred_element_type=F32)
    parity = jnp.where(jnp.arange(2 * length) % length < length // 2, 1.0, -1.0)[None, :, None]
    before = jnp.concatenate([jnp.zeros_like(data[:1]), data[:-1]], axis=0)
    pair = before + parity * data
    edge = (jnp.arange(length) == 0)[None, :, None]
    real = jnp.zeros_like(data[:, :length])
    imag = jnp.zeros_like(real)
    for lag in range(min(win, spans)):
        own = jnp.concatenate([jnp.zeros_like(pair[:lag]), pair[: spans - lag]], axis=0)
        own_real, own_imag = own[:, :length], own[:, length:]
        tap_real, tap_imag = block[lag, :length][None], block[lag, length:][None]
        first, second = tap_real * own_real, tap_imag * own_imag
        real = real + jnp.where(edge, first, first - second)
        imag = imag + jnp.where(edge, second, tap_real * own_imag + tap_imag * own_real)
    total = jnp.concatenate([real, imag], axis=1).astype(BF16)
    return jnp.einsum("im,kmc->kic", inverse, total, preferred_element_type=F32)


def plain_body(forward, inverse, query_gate, key_gate, value_in, filter_taps, skip_gain, out_weight):
    length, width = query_gate.shape
    devices = lax.axis_size("ctx")
    share = width // devices
    mixed_in = (key_gate.astype(F32) * value_in.astype(F32)).astype(BF16)
    x = lax.all_to_all(mixed_in, "ctx", split_axis=1, concat_axis=0, tiled=True)
    taps = lax.dynamic_slice_in_dim(filter_taps, lax.axis_index("ctx") * share, share, axis=1)
    conv = long_conv(
        x.reshape(devices, length, share),
        taps.astype(BF16).reshape(-1, length, share),
        forward,
        inverse,
    )
    conv = conv.astype(BF16).reshape(devices * length, share)
    conv = lax.all_to_all(conv, "ctx", split_axis=0, concat_axis=1, tiled=True)
    combined = conv.astype(F32) + skip_gain[None, :] * mixed_in.astype(F32)
    gated = (query_gate.astype(F32) * combined).astype(BF16)
    partial_value = jnp.dot(gated, out_weight, preferred_element_type=F32)
    return lax.psum_scatter(partial_value.astype(BF16), "ch", scatter_dimension=1, tiled=True)


MESH = pl.DeviceIdType.MESH
EIGHTHS = (2, 2, 2, 2)
AHEAD = 2
ROWS = 8


def spectral_tile(row, sign, edge, outs, ins, add, taps_ref, data_ref, total_ref):
    pairs, height, lanes = data_ref.shape
    share, lags = lanes // 2, 2 * taps_ref.shape[0]
    real_rows, imag_rows = pl.ds(row, ROWS), pl.ds(row + height // 2, ROWS)

    def parts(ref, index):
        cols = slice((index % 2) * share, (index % 2 + 1) * share)
        return ref[index // 2, real_rows, cols], ref[index // 2, imag_rows, cols]

    used = sorted({o - i for o in outs for i in ins if 0 <= o - i < lags})
    taps = {lag: parts(taps_ref, lag) for lag in used}
    own = {}
    before = parts(data_ref, ins[0] - 1) if ins[0] > 0 else None
    for span in ins:
        here = parts(data_ref, span)
        if before is None:
            own[span] = here if sign > 0 else tuple(-part for part in here)
        elif sign > 0:
            own[span] = tuple(b + h for b, h in zip(before, here))
        else:
            own[span] = tuple(b - h for b, h in zip(before, here))
        before = here
    for out in outs:
        first = second = cross = None
        for span in ins:
            if not 0 <= out - span < lags:
                continue
            (tr, ti), (xr, xi) = taps[out - span], own[span]
            if first is None:
                first, second, cross = tr * xr, ti * xi, tr * xi + ti * xr
            else:
                first, second = first + tr * xr, second + ti * xi
                cross = cross + tr * xi + ti * xr
        cols = slice((out % 2) * share, (out % 2 + 1) * share)
        if first is None:
            if not add:
                total_ref[out // 2, real_rows, cols] = jnp.zeros((ROWS, share), F32)
                total_ref[out // 2, imag_rows, cols] = jnp.zeros((ROWS, share), F32)
            continue
        real, imag = first - second, cross
        if edge:
            at_edge = lax.broadcasted_iota(jnp.int32, real.shape, 0) == 0
            real, imag = jnp.where(at_edge, first, real), jnp.where(at_edge, second, imag)
        if add:
            real += total_ref[out // 2, real_rows, cols]
            imag += total_ref[out // 2, imag_rows, cols]
        total_ref[out // 2, real_rows, cols] = real
        total_ref[out // 2, imag_rows, cols] = imag


def spectral_sums(outs, ins, add, taps_ref, data_ref, total_ref):
    refs = (taps_ref, data_ref, total_ref)
    tiles = data_ref.shape[1] // 4 // ROWS
    spectral_tile(0, 1, True, outs, ins, add, *refs)

    def even(i, carry):
        spectral_tile(pl.multiple_of(i * ROWS, ROWS), 1, False, outs, ins, add, *refs)
        return carry

    def odd(i, carry):
        spectral_tile(pl.multiple_of(i * ROWS, ROWS), -1, False, outs, ins, add, *refs)
        return carry

    lax.fori_loop(1, tiles, even, 0)
    lax.fori_loop(tiles, 2 * tiles, odd, 0)


def chunk_rows(length):
    ends = np.cumsum((0,) + EIGHTHS) * (length // 8)
    return [slice(int(a), int(b)) for a, b in zip(ends[:-1], ends[1:])]


def fused_kernel(
    n, q_hbm, k_hbm, v_hbm, taps_hbm, skip_ref, w_hbm, fwd_hbm, inv_hbm, out_ref,
    q_ref, k_ref, v_ref, taps_ref, w_ref, fwd_ref, inv_ref,
    mixed, recv1, spec_b, spec_x, total, total_b, send2, recv2, gated, s1, r1, s2, r2, acc,
    load_sem, own1_sem, own2_sem, a_send, a_recv, b_send, b_recv, c_send, c_recv, d_send, d_recv,
):
    me, ch = lax.axis_index("ctx"), lax.axis_index("ch")
    y, core = ch // 2, ch % 2
    beside, across = y * 2 + 1 - core, (1 - y) * 2 + core
    opposite = (1 - y) * 2 + 1 - core
    length, width = q_hbm.shape
    share, group = width // n, n // 2
    chunks = chunk_rows(length)
    side = me // group
    here = [side * group + lax.rem(me + i, group) for i in range(group)]
    there = [(1 - side) * group + lax.rem(me + i, group) for i in range(group)]
    order = [there[0]]
    for i in range(1, group):
        order += [here[i], there[i]]

    def load(index, src, dst):
        copy = pltpu.make_async_copy(src, dst, load_sem.at[index])
        copy.start()
        return copy

    taps_cols = pl.ds(pl.multiple_of(me * share, share), share)
    load_k, load_v = load(0, k_hbm, k_ref), load(1, v_hbm, v_ref)
    load_fwd = load(2, fwd_hbm, fwd_ref)
    load_taps = load(3, taps_hbm.at[:, taps_cols], taps_ref)
    load_inv, load_q = load(4, inv_hbm, inv_ref), load(5, q_hbm, q_ref)
    load_w = [
        load(6 + i, w_hbm.at[:, pl.ds(pl.multiple_of(owner * width, width), width)], w_ref.at[i])
        for i, owner in enumerate((opposite, beside, across, ch))
    ]

    barrier = pltpu.get_barrier_semaphore()
    for peer in order:
        pl.semaphore_signal(barrier, inc=1, device_id={"ctx": peer}, device_id_type=MESH)
    for other in (beside, across):
        pl.semaphore_signal(barrier, inc=1, device_id={"ch": other}, device_id_type=MESH)

    load_k.wait()
    load_v.wait()
    for d in range(n):
        cols = slice(d * share, (d + 1) * share)
        mixed[d] = (k_ref[:, cols].astype(F32) * v_ref[:, cols].astype(F32)).astype(BF16)
    pl.semaphore_wait(barrier, n + 1)

    def half(index):
        return pl.ds(pl.multiple_of(lax.rem(index, 2) * share, share), share)

    sends = []
    for i, peer in enumerate(order):
        copy = pltpu.make_async_remote_copy(
            src_ref=mixed.at[peer],
            dst_ref=recv1.at[me // 2, :, half(me)],
            send_sem=a_send.at[i],
            recv_sem=a_recv.at[me],
            device_id={"ctx": peer},
            device_id_type=MESH,
        )
        copy.start()
        sends.append(copy)
    own = pltpu.make_async_copy(mixed.at[me], recv1.at[me // 2, :, half(me)], own1_sem)
    own.start()

    load_fwd.wait()
    load_taps.wait()
    for p in range(spec_b.shape[0]):
        blocks = [taps_ref[(2 * p + i) * length : (2 * p + i + 1) * length] for i in range(2)]
        spec_b[p] = jnp.dot(
            fwd_ref[...], jnp.concatenate(blocks, axis=1).astype(BF16), preferred_element_type=F32
        )
    own.wait()

    def spectrum(p):
        for src in (2 * p, 2 * p + 1):

            @pl.when(src != me)
            def _():
                cols = slice((src % 2) * share, (src % 2 + 1) * share)
                pltpu.make_async_remote_copy(
                    src_ref=mixed.at[src],
                    dst_ref=recv1.at[src // 2, :, cols],
                    send_sem=a_send.at[0],
                    recv_sem=a_recv.at[src],
                    device_id={"ctx": order[0]},
                    device_id_type=MESH,
                ).wait_recv()

        spec_x[p] = jnp.dot(fwd_ref[...], recv1[p], preferred_element_type=F32)

    def way_back(t, peer):
        return pltpu.make_async_remote_copy(
            src_ref=send2.at[peer, chunks[t]],
            dst_ref=recv2.at[chunks[t], taps_cols],
            send_sem=b_send.at[t, peer],
            recv_sem=b_recv.at[t, me],
            device_id={"ctx": peer},
            device_id_type=MESH,
        )

    def own_rows(t):
        return pltpu.make_async_copy(
            send2.at[me, chunks[t]], recv2.at[chunks[t], taps_cols], own2_sem.at[t]
        )

    def launch(t, which):
        @pl.when(side == which)
        def _():
            own_rows(t).start()

        @pl.when(side != which)
        def _():
            way_back(t, which * group + lax.rem(me, group)).start()

        for i in range(1, group):
            way_back(t, which * group + lax.rem(me + i, group)).start()

    def send_back(which):
        pairs = range(which * group // 2, (which + 1) * group // 2)
        for p in pairs:
            total_b[p] = total[p].astype(BF16)
        for t, rows in enumerate(chunks):
            for p in pairs:
                conv = jnp.dot(inv_ref[rows], total_b[p], preferred_element_type=F32).astype(BF16)
                send2[2 * p, rows] = conv[:, :share]
                send2[2 * p + 1, rows] = conv[:, share:]
            if t < AHEAD:
                launch(t, which)

    low, high = range(group), range(group, n)
    for p in range(group // 2):
        spectrum(p)
    spectral_sums(low, low, False, spec_b, spec_x, total)
    load_inv.wait()
    send_back(0)
    spectral_sums(high, low, False, spec_b, spec_x, total)
    for p in range(group // 2, group):
        spectrum(p)
    spectral_sums(high, high, True, spec_b, spec_x, total)
    send_back(1)

    def exchange(src, dst, out_sem, in_sem, other):
        copy = pltpu.make_async_remote_copy(
            src_ref=src,
            dst_ref=dst,
            send_sem=out_sem,
            recv_sem=in_sem,
            device_id={"ch": other},
            device_id_type=MESH,
        )
        copy.start()
        sends.append(copy)
        return copy

    def project(rows, block):
        return jnp.dot(gated[rows], w_ref[block], preferred_element_type=F32)

    def finish(t, copy):
        copy.wait_recv()
        out_ref[chunks[t]] = (acc[chunks[t]] + r2[chunks[t]].astype(F32)).astype(BF16)

    load_q.wait()
    for copy in load_w:
        copy.wait()
    last = None
    for t, rows in enumerate(chunks):
        own_rows(t).wait()
        for src in range(n):

            @pl.when(src != me)
            def _():
                cols = slice(src * share, (src + 1) * share)
                pltpu.make_async_remote_copy(
                    src_ref=send2.at[src, rows],
                    dst_ref=recv2.at[rows, cols],
                    send_sem=b_send.at[t, src],
                    recv_sem=b_recv.at[t, src],
                    device_id={"ctx": order[0]},
                    device_id_type=MESH,
                ).wait_recv()

        for d in range(n):
            cols = slice(d * share, (d + 1) * share)
            conv = recv2[rows, cols].astype(F32)
            conv = conv + skip_ref[:, cols] * mixed[d, rows].astype(F32)
            gated[rows, cols] = (q_ref[rows, cols].astype(F32) * conv).astype(BF16)
        s1[0, rows] = project(rows, 0).astype(BF16)
        far = exchange(s1.at[0, rows], r1.at[0, rows], c_send.at[t, 0], c_recv.at[t, 0], beside)
        s1[1, rows] = project(rows, 1).astype(BF16)
        near = exchange(s1.at[1, rows], r1.at[1, rows], c_send.at[t, 1], c_recv.at[t, 1], beside)
        if t + AHEAD < len(chunks):
            launch(t + AHEAD, 0)
            launch(t + AHEAD, 1)
        passed = project(rows, 2)
        far.wait_recv()
        s2[rows] = (passed + r1[0, rows].astype(F32)).astype(BF16)
        final = exchange(s2.at[rows], r2.at[rows], d_send.at[t], d_recv.at[t], across)
        kept = project(rows, 3)
        near.wait_recv()
        acc[rows] = kept + r1[1, rows].astype(F32)
        if last is not None:
            finish(t - 1, last)
        last = final
    finish(len(chunks) - 1, last)
    for copy in sends:
        copy.wait_send()
    for t in range(len(chunks)):
        for i in range(1, group):
            way_back(t, here[i]).wait_send()
        for peer in there:
            way_back(t, peer).wait_send()


def fused_body(forward, inverse, query_gate, key_gate, value_in, filter_taps, skip_gain, out_weight):
    length, width = query_gate.shape
    n = lax.axis_size("ctx")
    share, taps, chunks = width // n, filter_taps.shape[0], len(EIGHTHS)
    dma = pltpu.SemaphoreType.DMA
    anywhere = pl.BlockSpec(memory_space=pl.ANY)
    vmem = pl.BlockSpec(memory_space=pltpu.VMEM)
    return pl.pallas_call(
        functools.partial(fused_kernel, n),
        out_shape=jax.ShapeDtypeStruct((length, width), BF16),
        in_specs=[anywhere] * 4 + [vmem] + [anywhere] * 3,
        out_specs=vmem,
        scratch_shapes=[
            pltpu.VMEM((length, width), BF16),
            pltpu.VMEM((length, width), BF16),
            pltpu.VMEM((length, width), BF16),
            pltpu.VMEM((taps, share), F32),
            pltpu.VMEM((4, width, width), BF16),
            pltpu.VMEM((2 * length, length), BF16),
            pltpu.VMEM((length, 2 * length), BF16),
            pltpu.VMEM((n, length, share), BF16),
            pltpu.VMEM((n // 2, length, 2 * share), BF16),
            pltpu.VMEM((taps // length // 2, 2 * length, 2 * share), F32),
            pltpu.VMEM((n // 2, 2 * length, 2 * share), F32),
            pltpu.VMEM((n // 2, 2 * length, 2 * share), F32),
            pltpu.VMEM((n // 2, 2 * length, 2 * share), BF16),
            pltpu.VMEM((n, length, share), BF16),
            pltpu.VMEM((length, width), BF16),
            pltpu.VMEM((length, width), BF16),
            pltpu.VMEM((2, length, width), BF16),
            pltpu.VMEM((2, length, width), BF16),
            pltpu.VMEM((length, width), BF16),
            pltpu.VMEM((length, width), BF16),
            pltpu.VMEM((length, width), F32),
            dma((10,)),
            dma,
            dma((chunks,)),
            dma((n - 1,)),
            dma((n,)),
            dma((chunks, n)),
            dma((chunks, n)),
            dma((chunks, 2)),
            dma((chunks, 2)),
            dma((chunks,)),
            dma((chunks,)),
        ],
        compiler_params=pltpu.CompilerParams(
            collective_id=0, has_side_effects=True, vmem_limit_bytes=56 * 2**20
        ),
        cost_estimate=pl.CostEstimate(
            flops=10 * 10**9, bytes_accessed=16 * 2**20, transcendentals=0
        ),
    )(
        query_gate, key_gate, value_in, filter_taps, skip_gain.reshape(1, width), out_weight,
        forward, inverse,
    )


def solution(mesh):
    in_specs = (
        P("ctx", "ch"),
        P("ctx", "ch"),
        P("ctx", "ch"),
        P(None, "ch"),
        P("ch"),
        P("ch", None),
    )
    out_specs = P("ctx", "ch")

    def whole(query_gate, *rest):
        length = query_gate.shape[0] // mesh.shape["ctx"]
        width = query_gate.shape[1] // mesh.shape["ch"]
        forward, inverse = transform_tables(length)
        taps = rest[2].shape[0] // length
        fits = mesh.shape["ch"] == 4 and width == 128 * mesh.shape["ctx"]
        fits = fits and mesh.shape["ctx"] % 4 == 0 and taps % 2 == 0 and length % 128 == 0
        chosen = fused_body if fits else plain_body

        def body(*args):
            return chosen(jnp.asarray(forward), jnp.asarray(inverse), *args)

        return jax.shard_map(
            body, mesh=mesh, in_specs=in_specs, out_specs=out_specs, check_vma=False
        )(query_gate, *rest)

    return whole
```

```python
import functools

import ml_dtypes
import numpy as np

import jax
import jax.numpy as jnp
from jax import lax
from jax.experimental import pallas as pl
from jax.experimental.pallas import tpu as pltpu
from jax.sharding import PartitionSpec as P

BF16 = jnp.bfloat16
F32 = jnp.float32


def transform_tables(length):
    freqs = np.concatenate([np.arange(0, length, 2), np.arange(1, length, 2)])[:, None]
    times = np.arange(length)[None, :]
    angle = (freqs * times % (2 * length)) * (np.pi / length)
    real, imag = np.cos(angle), -np.sin(angle)
    imag[0] = 1.0 - 2.0 * (np.arange(length) % 2)
    forward = np.concatenate([real, imag], axis=0)
    angle = (freqs * (times + length) % (2 * length)) * (np.pi / length)
    real, imag = np.cos(angle) / length, -np.sin(angle) / length
    real[0] = 0.5 / length
    imag[0] = (1.0 - 2.0 * ((np.arange(length) + length) % 2)) * 0.5 / length
    inverse = np.concatenate([real, imag], axis=0).T
    return forward.astype(ml_dtypes.bfloat16), inverse.astype(ml_dtypes.bfloat16)


def long_conv(x, taps, forward, inverse):
    spans, length, _ = x.shape
    win = taps.shape[0]
    data = jnp.einsum("mn,knc->kmc", forward, x, preferred_element_type=F32)
    block = jnp.einsum("mn,knc->kmc", forward, taps, preferred_element_type=F32)
    parity = jnp.where(jnp.arange(2 * length) % length < length // 2, 1.0, -1.0)[None, :, None]
    before = jnp.concatenate([jnp.zeros_like(data[:1]), data[:-1]], axis=0)
    pair = before + parity * data
    edge = (jnp.arange(length) == 0)[None, :, None]
    real = jnp.zeros_like(data[:, :length])
    imag = jnp.zeros_like(real)
    for lag in range(min(win, spans)):
        own = jnp.concatenate([jnp.zeros_like(pair[:lag]), pair[: spans - lag]], axis=0)
        own_real, own_imag = own[:, :length], own[:, length:]
        tap_real, tap_imag = block[lag, :length][None], block[lag, length:][None]
        first, second = tap_real * own_real, tap_imag * own_imag
        real = real + jnp.where(edge, first, first - second)
        imag = imag + jnp.where(edge, second, tap_real * own_imag + tap_imag * own_real)
    total = jnp.concatenate([real, imag], axis=1).astype(BF16)
    return jnp.einsum("im,kmc->kic", inverse, total, preferred_element_type=F32)


def plain_body(forward, inverse, query_gate, key_gate, value_in, filter_taps, skip_gain, out_weight):
    length, width = query_gate.shape
    devices = lax.axis_size("ctx")
    share = width // devices
    mixed_in = (key_gate.astype(F32) * value_in.astype(F32)).astype(BF16)
    x = lax.all_to_all(mixed_in, "ctx", split_axis=1, concat_axis=0, tiled=True)
    taps = lax.dynamic_slice_in_dim(filter_taps, lax.axis_index("ctx") * share, share, axis=1)
    conv = long_conv(
        x.reshape(devices, length, share),
        taps.astype(BF16).reshape(-1, length, share),
        forward,
        inverse,
    )
    conv = conv.astype(BF16).reshape(devices * length, share)
    conv = lax.all_to_all(conv, "ctx", split_axis=0, concat_axis=1, tiled=True)
    combined = conv.astype(F32) + skip_gain[None, :] * mixed_in.astype(F32)
    gated = (query_gate.astype(F32) * combined).astype(BF16)
    partial_value = jnp.dot(gated, out_weight, preferred_element_type=F32)
    return lax.psum_scatter(partial_value.astype(BF16), "ch", scatter_dimension=1, tiled=True)


MESH = pl.DeviceIdType.MESH
EIGHTHS = (2, 2, 2, 2)
AHEAD = 2
ROWS = 8


def spectral_tile(row, sign, edge, outs, ins, add, taps_ref, data_ref, total_ref):
    pairs, height, lanes = data_ref.shape
    share, lags = lanes // 2, 2 * taps_ref.shape[0]
    real_rows, imag_rows = pl.ds(row, ROWS), pl.ds(row + height // 2, ROWS)

    def parts(ref, index):
        cols = slice((index % 2) * share, (index % 2 + 1) * share)
        return ref[index // 2, real_rows, cols], ref[index // 2, imag_rows, cols]

    used = sorted({o - i for o in outs for i in ins if 0 <= o - i < lags})
    taps = {lag: parts(taps_ref, lag) for lag in used}
    own = {}
    before = parts(data_ref, ins[0] - 1) if ins[0] > 0 else None
    for span in ins:
        here = parts(data_ref, span)
        if before is None:
            own[span] = here if sign > 0 else tuple(-part for part in here)
        elif sign > 0:
            own[span] = tuple(b + h for b, h in zip(before, here))
        else:
            own[span] = tuple(b - h for b, h in zip(before, here))
        before = here
    for out in outs:
        first = second = cross = None
        for span in ins:
            if not 0 <= out - span < lags:
                continue
            (tr, ti), (xr, xi) = taps[out - span], own[span]
            if first is None:
                first, second, cross = tr * xr, ti * xi, tr * xi + ti * xr
            else:
                first, second = first + tr * xr, second + ti * xi
                cross = cross + tr * xi + ti * xr
        cols = slice((out % 2) * share, (out % 2 + 1) * share)
        if first is None:
            if not add:
                total_ref[out // 2, real_rows, cols] = jnp.zeros((ROWS, share), F32)
                total_ref[out // 2, imag_rows, cols] = jnp.zeros((ROWS, share), F32)
            continue
        real, imag = first - second, cross
        if edge:
            at_edge = lax.broadcasted_iota(jnp.int32, real.shape, 0) == 0
            real, imag = jnp.where(at_edge, first, real), jnp.where(at_edge, second, imag)
        if add:
            real += total_ref[out // 2, real_rows, cols]
            imag += total_ref[out // 2, imag_rows, cols]
        total_ref[out // 2, real_rows, cols] = real
        total_ref[out // 2, imag_rows, cols] = imag


def spectral_sums(outs, ins, add, taps_ref, data_ref, total_ref):
    refs = (taps_ref, data_ref, total_ref)
    tiles = data_ref.shape[1] // 4 // ROWS
    spectral_tile(0, 1, True, outs, ins, add, *refs)

    def even(i, carry):
        spectral_tile(pl.multiple_of(i * ROWS, ROWS), 1, False, outs, ins, add, *refs)
        return carry

    def odd(i, carry):
        spectral_tile(pl.multiple_of(i * ROWS, ROWS), -1, False, outs, ins, add, *refs)
        return carry

    lax.fori_loop(1, tiles, even, 0)
    lax.fori_loop(tiles, 2 * tiles, odd, 0)


def chunk_rows(length):
    ends = np.cumsum((0,) + EIGHTHS) * (length // 8)
    return [slice(int(a), int(b)) for a, b in zip(ends[:-1], ends[1:])]


def fused_kernel(
    n, q_hbm, k_hbm, v_hbm, taps_hbm, skip_ref, w_hbm, fwd_hbm, inv_hbm, out_ref,
    q_ref, k_ref, v_ref, taps_ref, w_ref, fwd_ref, inv_ref,
    mixed, recv1, spec_b, spec_x, total, total_b, send2, recv2, gated, s1, r1, s2, r2, acc,
    load_sem, own1_sem, own2_sem, a_send, a_recv, b_send, b_recv, c_send, c_recv, d_send, d_recv,
):
    me, ch = lax.axis_index("ctx"), lax.axis_index("ch")
    y, core = ch // 2, ch % 2
    beside, across = y * 2 + 1 - core, (1 - y) * 2 + core
    opposite = (1 - y) * 2 + 1 - core
    length, width = q_hbm.shape
    share, group = width // n, n // 2
    chunks = chunk_rows(length)
    side = me // group
    here = [side * group + lax.rem(me + i, group) for i in range(group)]
    there = [(1 - side) * group + lax.rem(me + i, group) for i in range(group)]
    order = [there[0]]
    for i in range(1, group):
        order += [here[i], there[i]]

    def load(index, src, dst):
        copy = pltpu.make_async_copy(src, dst, load_sem.at[index])
        copy.start()
        return copy

    taps_cols = pl.ds(pl.multiple_of(me * share, share), share)
    load_k, load_v = load(0, k_hbm, k_ref), load(1, v_hbm, v_ref)
    load_fwd = load(2, fwd_hbm, fwd_ref)
    load_taps = load(3, taps_hbm.at[:, taps_cols], taps_ref)
    load_inv, load_q = load(4, inv_hbm, inv_ref), load(5, q_hbm, q_ref)
    load_w = [
        load(6 + i, w_hbm.at[:, pl.ds(pl.multiple_of(owner * width, width), width)], w_ref.at[i])
        for i, owner in enumerate((opposite, beside, across, ch))
    ]

    barrier = pltpu.get_barrier_semaphore()
    for peer in order:
        pl.semaphore_signal(barrier, inc=1, device_id={"ctx": peer}, device_id_type=MESH)
    for other in (beside, across):
        pl.semaphore_signal(barrier, inc=1, device_id={"ch": other}, device_id_type=MESH)

    load_k.wait()
    load_v.wait()
    for d in range(n):
        cols = slice(d * share, (d + 1) * share)
        mixed[d] = (k_ref[:, cols].astype(F32) * v_ref[:, cols].astype(F32)).astype(BF16)
    pl.semaphore_wait(barrier, n + 1)

    def half(index):
        return pl.ds(pl.multiple_of(lax.rem(index, 2) * share, share), share)

    sends = []
    for i, peer in enumerate(order):
        copy = pltpu.make_async_remote_copy(
            src_ref=mixed.at[peer],
            dst_ref=recv1.at[me // 2, :, half(me)],
            send_sem=a_send.at[i],
            recv_sem=a_recv.at[me],
            device_id={"ctx": peer},
            device_id_type=MESH,
        )
        copy.start()
        sends.append(copy)
    own = pltpu.make_async_copy(mixed.at[me], recv1.at[me // 2, :, half(me)], own1_sem)
    own.start()

    load_fwd.wait()
    load_taps.wait()
    for p in range(spec_b.shape[0]):
        blocks = [taps_ref[(2 * p + i) * length : (2 * p + i + 1) * length] for i in range(2)]
        spec_b[p] = jnp.dot(
            fwd_ref[...], jnp.concatenate(blocks, axis=1).astype(BF16), preferred_element_type=F32
        )
    own.wait()

    def spectrum(p):
        for src in (2 * p, 2 * p + 1):

            @pl.when(src != me)
            def _():
                cols = slice((src % 2) * share, (src % 2 + 1) * share)
                pltpu.make_async_remote_copy(
                    src_ref=mixed.at[src],
                    dst_ref=recv1.at[src // 2, :, cols],
                    send_sem=a_send.at[0],
                    recv_sem=a_recv.at[src],
                    device_id={"ctx": order[0]},
                    device_id_type=MESH,
                ).wait_recv()

        spec_x[p] = jnp.dot(fwd_ref[...], recv1[p], preferred_element_type=F32)

    def way_back(t, peer):
        return pltpu.make_async_remote_copy(
            src_ref=send2.at[peer, chunks[t]],
            dst_ref=recv2.at[chunks[t], taps_cols],
            send_sem=b_send.at[t, peer],
            recv_sem=b_recv.at[t, me],
            device_id={"ctx": peer},
            device_id_type=MESH,
        )

    def own_rows(t):
        return pltpu.make_async_copy(
            send2.at[me, chunks[t]], recv2.at[chunks[t], taps_cols], own2_sem.at[t]
        )

    def launch(t, which):
        @pl.when(side == which)
        def _():
            own_rows(t).start()

        @pl.when(side != which)
        def _():
            way_back(t, which * group + lax.rem(me, group)).start()

        for i in range(1, group):
            way_back(t, which * group + lax.rem(me + i, group)).start()

    def send_back(which):
        pairs = range(which * group // 2, (which + 1) * group // 2)
        for p in pairs:
            total_b[p] = total[p].astype(BF16)
        for t, rows in enumerate(chunks):
            for p in pairs:
                conv = jnp.dot(inv_ref[rows], total_b[p], preferred_element_type=F32).astype(BF16)
                send2[2 * p, rows] = conv[:, :share]
                send2[2 * p + 1, rows] = conv[:, share:]
            if t < AHEAD:
                launch(t, which)

    low, high = range(group), range(group, n)
    for p in range(group // 2):
        spectrum(p)
    spectral_sums(low, low, False, spec_b, spec_x, total)
    load_inv.wait()
    send_back(0)
    spectral_sums(high, low, False, spec_b, spec_x, total)
    for p in range(group // 2, group):
        spectrum(p)
    spectral_sums(high, high, True, spec_b, spec_x, total)
    send_back(1)

    def exchange(src, dst, out_sem, in_sem, other):
        copy = pltpu.make_async_remote_copy(
            src_ref=src,
            dst_ref=dst,
            send_sem=out_sem,
            recv_sem=in_sem,
            device_id={"ch": other},
            device_id_type=MESH,
        )
        copy.start()
        sends.append(copy)
        return copy

    def project(rows, block):
        return jnp.dot(gated[rows], w_ref[block], preferred_element_type=F32)

    def finish(t, copy):
        copy.wait_recv()
        out_ref[chunks[t]] = (acc[chunks[t]] + r2[chunks[t]].astype(F32)).astype(BF16)

    load_q.wait()
    for copy in load_w:
        copy.wait()
    last = None
    for t, rows in enumerate(chunks):
        own_rows(t).wait()
        for src in range(n):

            @pl.when(src != me)
            def _():
                cols = slice(src * share, (src + 1) * share)
                pltpu.make_async_remote_copy(
                    src_ref=send2.at[src, rows],
                    dst_ref=recv2.at[rows, cols],
                    send_sem=b_send.at[t, src],
                    recv_sem=b_recv.at[t, src],
                    device_id={"ctx": order[0]},
                    device_id_type=MESH,
                ).wait_recv()

        for d in range(n):
            cols = slice(d * share, (d + 1) * share)
            conv = recv2[rows, cols].astype(F32)
            conv = conv + skip_ref[:, cols] * mixed[d, rows].astype(F32)
            gated[rows, cols] = (q_ref[rows, cols].astype(F32) * conv).astype(BF16)
        s1[0, rows] = project(rows, 0).astype(BF16)
        far = exchange(s1.at[0, rows], r1.at[0, rows], c_send.at[t, 0], c_recv.at[t, 0], beside)
        s1[1, rows] = project(rows, 1).astype(BF16)
        near = exchange(s1.at[1, rows], r1.at[1, rows], c_send.at[t, 1], c_recv.at[t, 1], beside)
        passed = project(rows, 2)
        far.wait_recv()
        s2[rows] = (passed + r1[0, rows].astype(F32)).astype(BF16)
        final = exchange(s2.at[rows], r2.at[rows], d_send.at[t], d_recv.at[t], across)
        if t + AHEAD < len(chunks):
            launch(t + AHEAD, 0)
            launch(t + AHEAD, 1)
        kept = project(rows, 3)
        near.wait_recv()
        acc[rows] = kept + r1[1, rows].astype(F32)
        if last is not None:
            finish(t - 1, last)
        last = final
    finish(len(chunks) - 1, last)
    for copy in sends:
        copy.wait_send()
    for t in range(len(chunks)):
        for i in range(1, group):
            way_back(t, here[i]).wait_send()
        for peer in there:
            way_back(t, peer).wait_send()


def fused_body(forward, inverse, query_gate, key_gate, value_in, filter_taps, skip_gain, out_weight):
    length, width = query_gate.shape
    n = lax.axis_size("ctx")
    share, taps, chunks = width // n, filter_taps.shape[0], len(EIGHTHS)
    dma = pltpu.SemaphoreType.DMA
    anywhere = pl.BlockSpec(memory_space=pl.ANY)
    vmem = pl.BlockSpec(memory_space=pltpu.VMEM)
    return pl.pallas_call(
        functools.partial(fused_kernel, n),
        out_shape=jax.ShapeDtypeStruct((length, width), BF16),
        in_specs=[anywhere] * 4 + [vmem] + [anywhere] * 3,
        out_specs=vmem,
        scratch_shapes=[
            pltpu.VMEM((length, width), BF16),
            pltpu.VMEM((length, width), BF16),
            pltpu.VMEM((length, width), BF16),
            pltpu.VMEM((taps, share), F32),
            pltpu.VMEM((4, width, width), BF16),
            pltpu.VMEM((2 * length, length), BF16),
            pltpu.VMEM((length, 2 * length), BF16),
            pltpu.VMEM((n, length, share), BF16),
            pltpu.VMEM((n // 2, length, 2 * share), BF16),
            pltpu.VMEM((taps // length // 2, 2 * length, 2 * share), F32),
            pltpu.VMEM((n // 2, 2 * length, 2 * share), F32),
            pltpu.VMEM((n // 2, 2 * length, 2 * share), F32),
            pltpu.VMEM((n // 2, 2 * length, 2 * share), BF16),
            pltpu.VMEM((n, length, share), BF16),
            pltpu.VMEM((length, width), BF16),
            pltpu.VMEM((length, width), BF16),
            pltpu.VMEM((2, length, width), BF16),
            pltpu.VMEM((2, length, width), BF16),
            pltpu.VMEM((length, width), BF16),
            pltpu.VMEM((length, width), BF16),
            pltpu.VMEM((length, width), F32),
            dma((10,)),
            dma,
            dma((chunks,)),
            dma((n - 1,)),
            dma((n,)),
            dma((chunks, n)),
            dma((chunks, n)),
            dma((chunks, 2)),
            dma((chunks, 2)),
            dma((chunks,)),
            dma((chunks,)),
        ],
        compiler_params=pltpu.CompilerParams(
            collective_id=0, has_side_effects=True, vmem_limit_bytes=56 * 2**20
        ),
        cost_estimate=pl.CostEstimate(
            flops=10 * 10**9, bytes_accessed=16 * 2**20, transcendentals=0
        ),
    )(
        query_gate, key_gate, value_in, filter_taps, skip_gain.reshape(1, width), out_weight,
        forward, inverse,
    )


def solution(mesh):
    in_specs = (
        P("ctx", "ch"),
        P("ctx", "ch"),
        P("ctx", "ch"),
        P(None, "ch"),
        P("ch"),
        P("ch", None),
    )
    out_specs = P("ctx", "ch")

    def whole(query_gate, *rest):
        length = query_gate.shape[0] // mesh.shape["ctx"]
        width = query_gate.shape[1] // mesh.shape["ch"]
        forward, inverse = transform_tables(length)
        taps = rest[2].shape[0] // length
        fits = mesh.shape["ch"] == 4 and width == 128 * mesh.shape["ctx"]
        fits = fits and mesh.shape["ctx"] % 4 == 0 and taps % 2 == 0 and length % 128 == 0
        chosen = fused_body if fits else plain_body

        def body(*args):
            return chosen(jnp.asarray(forward), jnp.asarray(inverse), *args)

        return jax.shard_map(
            body, mesh=mesh, in_specs=in_specs, out_specs=out_specs, check_vma=False
        )(query_gate, *rest)

    return whole
```

```python
import functools

import ml_dtypes
import numpy as np

import jax
import jax.numpy as jnp
from jax import lax
from jax.experimental import pallas as pl
from jax.experimental.pallas import tpu as pltpu
from jax.sharding import PartitionSpec as P

BF16 = jnp.bfloat16
F32 = jnp.float32


def transform_tables(length):
    freqs = np.concatenate([np.arange(0, length, 2), np.arange(1, length, 2)])[:, None]
    times = np.arange(length)[None, :]
    angle = (freqs * times % (2 * length)) * (np.pi / length)
    real, imag = np.cos(angle), -np.sin(angle)
    imag[0] = 1.0 - 2.0 * (np.arange(length) % 2)
    forward = np.concatenate([real, imag], axis=0)
    angle = (freqs * (times + length) % (2 * length)) * (np.pi / length)
    real, imag = np.cos(angle) / length, -np.sin(angle) / length
    real[0] = 0.5 / length
    imag[0] = (1.0 - 2.0 * ((np.arange(length) + length) % 2)) * 0.5 / length
    inverse = np.concatenate([real, imag], axis=0).T
    return forward.astype(ml_dtypes.bfloat16), inverse.astype(ml_dtypes.bfloat16)


def long_conv(x, taps, forward, inverse):
    spans, length, _ = x.shape
    win = taps.shape[0]
    data = jnp.einsum("mn,knc->kmc", forward, x, preferred_element_type=F32)
    block = jnp.einsum("mn,knc->kmc", forward, taps, preferred_element_type=F32)
    parity = jnp.where(jnp.arange(2 * length) % length < length // 2, 1.0, -1.0)[None, :, None]
    before = jnp.concatenate([jnp.zeros_like(data[:1]), data[:-1]], axis=0)
    pair = before + parity * data
    edge = (jnp.arange(length) == 0)[None, :, None]
    real = jnp.zeros_like(data[:, :length])
    imag = jnp.zeros_like(real)
    for lag in range(min(win, spans)):
        own = jnp.concatenate([jnp.zeros_like(pair[:lag]), pair[: spans - lag]], axis=0)
        own_real, own_imag = own[:, :length], own[:, length:]
        tap_real, tap_imag = block[lag, :length][None], block[lag, length:][None]
        first, second = tap_real * own_real, tap_imag * own_imag
        real = real + jnp.where(edge, first, first - second)
        imag = imag + jnp.where(edge, second, tap_real * own_imag + tap_imag * own_real)
    total = jnp.concatenate([real, imag], axis=1).astype(BF16)
    return jnp.einsum("im,kmc->kic", inverse, total, preferred_element_type=F32)


def plain_body(forward, inverse, query_gate, key_gate, value_in, filter_taps, skip_gain, out_weight):
    length, width = query_gate.shape
    devices = lax.axis_size("ctx")
    share = width // devices
    mixed_in = (key_gate.astype(F32) * value_in.astype(F32)).astype(BF16)
    x = lax.all_to_all(mixed_in, "ctx", split_axis=1, concat_axis=0, tiled=True)
    taps = lax.dynamic_slice_in_dim(filter_taps, lax.axis_index("ctx") * share, share, axis=1)
    conv = long_conv(
        x.reshape(devices, length, share),
        taps.astype(BF16).reshape(-1, length, share),
        forward,
        inverse,
    )
    conv = conv.astype(BF16).reshape(devices * length, share)
    conv = lax.all_to_all(conv, "ctx", split_axis=0, concat_axis=1, tiled=True)
    combined = conv.astype(F32) + skip_gain[None, :] * mixed_in.astype(F32)
    gated = (query_gate.astype(F32) * combined).astype(BF16)
    partial_value = jnp.dot(gated, out_weight, preferred_element_type=F32)
    return lax.psum_scatter(partial_value.astype(BF16), "ch", scatter_dimension=1, tiled=True)


MESH = pl.DeviceIdType.MESH
EIGHTHS = (1, 2, 2, 2, 1)
AHEAD = 2
ROWS = 8


def spectral_tile(row, sign, edge, outs, ins, add, taps_ref, data_ref, total_ref):
    pairs, height, lanes = data_ref.shape
    share, lags = lanes // 2, 2 * taps_ref.shape[0]
    real_rows, imag_rows = pl.ds(row, ROWS), pl.ds(row + height // 2, ROWS)

    def parts(ref, index):
        cols = slice((index % 2) * share, (index % 2 + 1) * share)
        return ref[index // 2, real_rows, cols], ref[index // 2, imag_rows, cols]

    used = sorted({o - i for o in outs for i in ins if 0 <= o - i < lags})
    taps = {lag: parts(taps_ref, lag) for lag in used}
    own = {}
    before = parts(data_ref, ins[0] - 1) if ins[0] > 0 else None
    for span in ins:
        here = parts(data_ref, span)
        if before is None:
            own[span] = here if sign > 0 else tuple(-part for part in here)
        elif sign > 0:
            own[span] = tuple(b + h for b, h in zip(before, here))
        else:
            own[span] = tuple(b - h for b, h in zip(before, here))
        before = here
    for out in outs:
        first = second = cross = None
        for span in ins:
            if not 0 <= out - span < lags:
                continue
            (tr, ti), (xr, xi) = taps[out - span], own[span]
            if first is None:
                first, second, cross = tr * xr, ti * xi, tr * xi + ti * xr
            else:
                first, second = first + tr * xr, second + ti * xi
                cross = cross + tr * xi + ti * xr
        cols = slice((out % 2) * share, (out % 2 + 1) * share)
        if first is None:
            if not add:
                total_ref[out // 2, real_rows, cols] = jnp.zeros((ROWS, share), F32)
                total_ref[out // 2, imag_rows, cols] = jnp.zeros((ROWS, share), F32)
            continue
        real, imag = first - second, cross
        if edge:
            at_edge = lax.broadcasted_iota(jnp.int32, real.shape, 0) == 0
            real, imag = jnp.where(at_edge, first, real), jnp.where(at_edge, second, imag)
        if add:
            real += total_ref[out // 2, real_rows, cols]
            imag += total_ref[out // 2, imag_rows, cols]
        total_ref[out // 2, real_rows, cols] = real
        total_ref[out // 2, imag_rows, cols] = imag


def spectral_sums(outs, ins, add, taps_ref, data_ref, total_ref):
    refs = (taps_ref, data_ref, total_ref)
    tiles = data_ref.shape[1] // 4 // ROWS
    spectral_tile(0, 1, True, outs, ins, add, *refs)

    def even(i, carry):
        spectral_tile(pl.multiple_of(i * ROWS, ROWS), 1, False, outs, ins, add, *refs)
        return carry

    def odd(i, carry):
        spectral_tile(pl.multiple_of(i * ROWS, ROWS), -1, False, outs, ins, add, *refs)
        return carry

    lax.fori_loop(1, tiles, even, 0)
    lax.fori_loop(tiles, 2 * tiles, odd, 0)


def chunk_rows(length):
    ends = np.cumsum((0,) + EIGHTHS) * (length // 8)
    return [slice(int(a), int(b)) for a, b in zip(ends[:-1], ends[1:])]


def fused_kernel(
    n, q_hbm, k_hbm, v_hbm, taps_hbm, skip_ref, w_hbm, fwd_hbm, inv_hbm, out_ref,
    q_ref, k_ref, v_ref, taps_ref, w_ref, fwd_ref, inv_ref,
    mixed, recv1, spec_b, spec_x, total, total_b, send2, recv2, gated, s1, r1, s2, r2, acc,
    load_sem, own1_sem, own2_sem, a_send, a_recv, b_send, b_recv, c_send, c_recv, d_send, d_recv,
):
    me, ch = lax.axis_index("ctx"), lax.axis_index("ch")
    y, core = ch // 2, ch % 2
    beside, across = y * 2 + 1 - core, (1 - y) * 2 + core
    opposite = (1 - y) * 2 + 1 - core
    length, width = q_hbm.shape
    share, group = width // n, n // 2
    chunks = chunk_rows(length)
    side = me // group
    here = [side * group + lax.rem(me + i, group) for i in range(group)]
    there = [(1 - side) * group + lax.rem(me + i, group) for i in range(group)]
    order = [there[0]]
    for i in range(1, group):
        order += [here[i], there[i]]

    def load(index, src, dst):
        copy = pltpu.make_async_copy(src, dst, load_sem.at[index])
        copy.start()
        return copy

    taps_cols = pl.ds(pl.multiple_of(me * share, share), share)
    load_k, load_v = load(0, k_hbm, k_ref), load(1, v_hbm, v_ref)
    load_fwd = load(2, fwd_hbm, fwd_ref)
    load_taps = load(3, taps_hbm.at[:, taps_cols], taps_ref)
    load_inv, load_q = load(4, inv_hbm, inv_ref), load(5, q_hbm, q_ref)
    load_w = [
        load(6 + i, w_hbm.at[:, pl.ds(pl.multiple_of(owner * width, width), width)], w_ref.at[i])
        for i, owner in enumerate((opposite, beside, across, ch))
    ]

    barrier = pltpu.get_barrier_semaphore()
    for peer in order:
        pl.semaphore_signal(barrier, inc=1, device_id={"ctx": peer}, device_id_type=MESH)
    for other in (beside, across):
        pl.semaphore_signal(barrier, inc=1, device_id={"ch": other}, device_id_type=MESH)

    load_k.wait()
    load_v.wait()
    for d in range(n):
        cols = slice(d * share, (d + 1) * share)
        mixed[d] = (k_ref[:, cols].astype(F32) * v_ref[:, cols].astype(F32)).astype(BF16)
    pl.semaphore_wait(barrier, n + 1)

    def half(index):
        return pl.ds(pl.multiple_of(lax.rem(index, 2) * share, share), share)

    sends = []
    for i, peer in enumerate(order):
        copy = pltpu.make_async_remote_copy(
            src_ref=mixed.at[peer],
            dst_ref=recv1.at[me // 2, :, half(me)],
            send_sem=a_send.at[i],
            recv_sem=a_recv.at[me],
            device_id={"ctx": peer},
            device_id_type=MESH,
        )
        copy.start()
        sends.append(copy)
    own = pltpu.make_async_copy(mixed.at[me], recv1.at[me // 2, :, half(me)], own1_sem)
    own.start()

    load_fwd.wait()
    load_taps.wait()
    for p in range(spec_b.shape[0]):
        blocks = [taps_ref[(2 * p + i) * length : (2 * p + i + 1) * length] for i in range(2)]
        spec_b[p] = jnp.dot(
            fwd_ref[...], jnp.concatenate(blocks, axis=1).astype(BF16), preferred_element_type=F32
        )
    own.wait()

    def spectrum(p):
        for src in (2 * p, 2 * p + 1):

            @pl.when(src != me)
            def _():
                cols = slice((src % 2) * share, (src % 2 + 1) * share)
                pltpu.make_async_remote_copy(
                    src_ref=mixed.at[src],
                    dst_ref=recv1.at[src // 2, :, cols],
                    send_sem=a_send.at[0],
                    recv_sem=a_recv.at[src],
                    device_id={"ctx": order[0]},
                    device_id_type=MESH,
                ).wait_recv()

        spec_x[p] = jnp.dot(fwd_ref[...], recv1[p], preferred_element_type=F32)

    def way_back(t, peer):
        return pltpu.make_async_remote_copy(
            src_ref=send2.at[peer, chunks[t]],
            dst_ref=recv2.at[chunks[t], taps_cols],
            send_sem=b_send.at[t, peer],
            recv_sem=b_recv.at[t, me],
            device_id={"ctx": peer},
            device_id_type=MESH,
        )

    def own_rows(t):
        return pltpu.make_async_copy(
            send2.at[me, chunks[t]], recv2.at[chunks[t], taps_cols], own2_sem.at[t]
        )

    def launch(t, which):
        @pl.when(side == which)
        def _():
            own_rows(t).start()

        @pl.when(side != which)
        def _():
            way_back(t, which * group + lax.rem(me, group)).start()

        for i in range(1, group):
            way_back(t, which * group + lax.rem(me + i, group)).start()

    def send_back(which):
        pairs = range(which * group // 2, (which + 1) * group // 2)
        for p in pairs:
            total_b[p] = total[p].astype(BF16)
        for t, rows in enumerate(chunks):
            for p in pairs:
                conv = jnp.dot(inv_ref[rows], total_b[p], preferred_element_type=F32).astype(BF16)
                send2[2 * p, rows] = conv[:, :share]
                send2[2 * p + 1, rows] = conv[:, share:]
            if t < AHEAD:
                launch(t, which)

    low, high = range(group), range(group, n)
    for p in range(group // 2):
        spectrum(p)
    spectral_sums(low, low, False, spec_b, spec_x, total)
    load_inv.wait()
    send_back(0)
    spectral_sums(high, low, False, spec_b, spec_x, total)
    for p in range(group // 2, group):
        spectrum(p)
    spectral_sums(high, high, True, spec_b, spec_x, total)
    send_back(1)

    def exchange(src, dst, out_sem, in_sem, other):
        copy = pltpu.make_async_remote_copy(
            src_ref=src,
            dst_ref=dst,
            send_sem=out_sem,
            recv_sem=in_sem,
            device_id={"ch": other},
            device_id_type=MESH,
        )
        copy.start()
        sends.append(copy)
        return copy

    def project(rows, block):
        return jnp.dot(gated[rows], w_ref[block], preferred_element_type=F32)

    def finish(t, copy):
        copy.wait_recv()
        out_ref[chunks[t]] = (acc[chunks[t]] + r2[chunks[t]].astype(F32)).astype(BF16)

    load_q.wait()
    for copy in load_w:
        copy.wait()
    last = None
    for t, rows in enumerate(chunks):
        own_rows(t).wait()
        for src in range(n):

            @pl.when(src != me)
            def _():
                cols = slice(src * share, (src + 1) * share)
                pltpu.make_async_remote_copy(
                    src_ref=send2.at[src, rows],
                    dst_ref=recv2.at[rows, cols],
                    send_sem=b_send.at[t, src],
                    recv_sem=b_recv.at[t, src],
                    device_id={"ctx": order[0]},
                    device_id_type=MESH,
                ).wait_recv()

        for d in range(n):
            cols = slice(d * share, (d + 1) * share)
            conv = recv2[rows, cols].astype(F32)
            conv = conv + skip_ref[:, cols] * mixed[d, rows].astype(F32)
            gated[rows, cols] = (q_ref[rows, cols].astype(F32) * conv).astype(BF16)
        s1[0, rows] = project(rows, 0).astype(BF16)
        far = exchange(s1.at[0, rows], r1.at[0, rows], c_send.at[t, 0], c_recv.at[t, 0], beside)
        s1[1, rows] = project(rows, 1).astype(BF16)
        near = exchange(s1.at[1, rows], r1.at[1, rows], c_send.at[t, 1], c_recv.at[t, 1], beside)
        if t + AHEAD < len(chunks):
            launch(t + AHEAD, 0)
            launch(t + AHEAD, 1)
        passed = project(rows, 2)
        far.wait_recv()
        s2[rows] = (passed + r1[0, rows].astype(F32)).astype(BF16)
        final = exchange(s2.at[rows], r2.at[rows], d_send.at[t], d_recv.at[t], across)
        kept = project(rows, 3)
        near.wait_recv()
        acc[rows] = kept + r1[1, rows].astype(F32)
        if last is not None:
            finish(t - 1, last)
        last = final
    finish(len(chunks) - 1, last)
    for copy in sends:
        copy.wait_send()
    for t in range(len(chunks)):
        for i in range(1, group):
            way_back(t, here[i]).wait_send()
        for peer in there:
            way_back(t, peer).wait_send()


def hand_over_kernel(src_hbm, out_hbm, sems):
    rows = src_hbm.shape[0] // 8
    copies = []
    for i in range(8):
        piece = slice(i * rows, (i + 1) * rows)
        copy = pltpu.make_async_copy(src_hbm.at[piece], out_hbm.at[piece], sems.at[i])
        copy.start()
        copies.append(copy)
    for copy in copies:
        copy.wait()


def hand_over(result):
    anywhere = pl.BlockSpec(memory_space=pl.ANY)
    return pl.pallas_call(
        hand_over_kernel,
        out_shape=jax.ShapeDtypeStruct(result.shape, result.dtype),
        in_specs=[anywhere],
        out_specs=anywhere,
        scratch_shapes=[pltpu.SemaphoreType.DMA((8,))],
    )(result)


def fused_body(forward, inverse, query_gate, key_gate, value_in, filter_taps, skip_gain, out_weight):
    length, width = query_gate.shape
    n = lax.axis_size("ctx")
    share, taps, chunks = width // n, filter_taps.shape[0], len(EIGHTHS)
    dma = pltpu.SemaphoreType.DMA
    anywhere = pl.BlockSpec(memory_space=pl.ANY)
    vmem = pl.BlockSpec(memory_space=pltpu.VMEM)
    result = pl.pallas_call(
        functools.partial(fused_kernel, n),
        out_shape=jax.ShapeDtypeStruct((length, width), BF16),
        in_specs=[anywhere] * 4 + [vmem] + [anywhere] * 3,
        out_specs=vmem,
        scratch_shapes=[
            pltpu.VMEM((length, width), BF16),
            pltpu.VMEM((length, width), BF16),
            pltpu.VMEM((length, width), BF16),
            pltpu.VMEM((taps, share), F32),
            pltpu.VMEM((4, width, width), BF16),
            pltpu.VMEM((2 * length, length), BF16),
            pltpu.VMEM((length, 2 * length), BF16),
            pltpu.VMEM((n, length, share), BF16),
            pltpu.VMEM((n // 2, length, 2 * share), BF16),
            pltpu.VMEM((taps // length // 2, 2 * length, 2 * share), F32),
            pltpu.VMEM((n // 2, 2 * length, 2 * share), F32),
            pltpu.VMEM((n // 2, 2 * length, 2 * share), F32),
            pltpu.VMEM((n // 2, 2 * length, 2 * share), BF16),
            pltpu.VMEM((n, length, share), BF16),
            pltpu.VMEM((length, width), BF16),
            pltpu.VMEM((length, width), BF16),
            pltpu.VMEM((2, length, width), BF16),
            pltpu.VMEM((2, length, width), BF16),
            pltpu.VMEM((length, width), BF16),
            pltpu.VMEM((length, width), BF16),
            pltpu.VMEM((length, width), F32),
            dma((10,)),
            dma,
            dma((chunks,)),
            dma((n - 1,)),
            dma((n,)),
            dma((chunks, n)),
            dma((chunks, n)),
            dma((chunks, 2)),
            dma((chunks, 2)),
            dma((chunks,)),
            dma((chunks,)),
        ],
        compiler_params=pltpu.CompilerParams(
            collective_id=0, has_side_effects=True, vmem_limit_bytes=56 * 2**20
        ),
        cost_estimate=pl.CostEstimate(
            flops=10 * 10**9, bytes_accessed=16 * 2**20, transcendentals=0
        ),
    )(
        query_gate, key_gate, value_in, filter_taps, skip_gain.reshape(1, width), out_weight,
        forward, inverse,
    )
    return hand_over(result)


def solution(mesh):
    in_specs = (
        P("ctx", "ch"),
        P("ctx", "ch"),
        P("ctx", "ch"),
        P(None, "ch"),
        P("ch"),
        P("ch", None),
    )
    out_specs = P("ctx", "ch")

    def whole(query_gate, *rest):
        length = query_gate.shape[0] // mesh.shape["ctx"]
        width = query_gate.shape[1] // mesh.shape["ch"]
        forward, inverse = transform_tables(length)
        taps = rest[2].shape[0] // length
        fits = mesh.shape["ch"] == 4 and width == 128 * mesh.shape["ctx"]
        fits = fits and mesh.shape["ctx"] % 4 == 0 and taps % 2 == 0 and length % 128 == 0
        chosen = fused_body if fits else plain_body

        def body(*args):
            return chosen(jnp.asarray(forward), jnp.asarray(inverse), *args)

        return jax.shard_map(
            body, mesh=mesh, in_specs=in_specs, out_specs=out_specs, check_vma=False
        )(query_gate, *rest)

    return whole
```

```python
import functools

import ml_dtypes
import numpy as np

import jax
import jax.numpy as jnp
from jax import lax
from jax.experimental import pallas as pl
from jax.experimental.pallas import tpu as pltpu
from jax.sharding import PartitionSpec as P

BF16 = jnp.bfloat16
F32 = jnp.float32


def transform_tables(length):
    freqs = np.concatenate([np.arange(0, length, 2), np.arange(1, length, 2)])[:, None]
    times = np.arange(length)[None, :]
    angle = (freqs * times % (2 * length)) * (np.pi / length)
    real, imag = np.cos(angle), -np.sin(angle)
    imag[0] = 1.0 - 2.0 * (np.arange(length) % 2)
    forward = np.concatenate([real, imag], axis=0)
    angle = (freqs * (times + length) % (2 * length)) * (np.pi / length)
    real, imag = np.cos(angle) / length, -np.sin(angle) / length
    real[0] = 0.5 / length
    imag[0] = (1.0 - 2.0 * ((np.arange(length) + length) % 2)) * 0.5 / length
    inverse = np.concatenate([real, imag], axis=0).T
    return forward.astype(ml_dtypes.bfloat16), inverse.astype(ml_dtypes.bfloat16)


def long_conv(x, taps, forward, inverse):
    spans, length, _ = x.shape
    win = taps.shape[0]
    data = jnp.einsum("mn,knc->kmc", forward, x, preferred_element_type=F32)
    block = jnp.einsum("mn,knc->kmc", forward, taps, preferred_element_type=F32)
    parity = jnp.where(jnp.arange(2 * length) % length < length // 2, 1.0, -1.0)[None, :, None]
    before = jnp.concatenate([jnp.zeros_like(data[:1]), data[:-1]], axis=0)
    pair = before + parity * data
    edge = (jnp.arange(length) == 0)[None, :, None]
    real = jnp.zeros_like(data[:, :length])
    imag = jnp.zeros_like(real)
    for lag in range(min(win, spans)):
        own = jnp.concatenate([jnp.zeros_like(pair[:lag]), pair[: spans - lag]], axis=0)
        own_real, own_imag = own[:, :length], own[:, length:]
        tap_real, tap_imag = block[lag, :length][None], block[lag, length:][None]
        first, second = tap_real * own_real, tap_imag * own_imag
        real = real + jnp.where(edge, first, first - second)
        imag = imag + jnp.where(edge, second, tap_real * own_imag + tap_imag * own_real)
    total = jnp.concatenate([real, imag], axis=1).astype(BF16)
    return jnp.einsum("im,kmc->kic", inverse, total, preferred_element_type=F32)


def plain_body(forward, inverse, query_gate, key_gate, value_in, filter_taps, skip_gain, out_weight):
    length, width = query_gate.shape
    devices = lax.axis_size("ctx")
    share = width // devices
    mixed_in = (key_gate.astype(F32) * value_in.astype(F32)).astype(BF16)
    x = lax.all_to_all(mixed_in, "ctx", split_axis=1, concat_axis=0, tiled=True)
    taps = lax.dynamic_slice_in_dim(filter_taps, lax.axis_index("ctx") * share, share, axis=1)
    conv = long_conv(
        x.reshape(devices, length, share),
        taps.astype(BF16).reshape(-1, length, share),
        forward,
        inverse,
    )
    conv = conv.astype(BF16).reshape(devices * length, share)
    conv = lax.all_to_all(conv, "ctx", split_axis=0, concat_axis=1, tiled=True)
    combined = conv.astype(F32) + skip_gain[None, :] * mixed_in.astype(F32)
    gated = (query_gate.astype(F32) * combined).astype(BF16)
    partial_value = jnp.dot(gated, out_weight, preferred_element_type=F32)
    return lax.psum_scatter(partial_value.astype(BF16), "ch", scatter_dimension=1, tiled=True)


MESH = pl.DeviceIdType.MESH
EIGHTHS = (2, 2, 2, 2)
AHEAD = 2
ROWS = 8


def spectral_tile(row, sign, edge, outs, ins, add, taps_ref, data_ref, total_ref):
    pairs, height, lanes = data_ref.shape
    share, lags = lanes // 2, 2 * taps_ref.shape[0]
    real_rows, imag_rows = pl.ds(row, ROWS), pl.ds(row + height // 2, ROWS)

    def parts(ref, index):
        cols = slice((index % 2) * share, (index % 2 + 1) * share)
        return ref[index // 2, real_rows, cols], ref[index // 2, imag_rows, cols]

    used = sorted({o - i for o in outs for i in ins if 0 <= o - i < lags})
    taps = {lag: parts(taps_ref, lag) for lag in used}
    own = {}
    before = parts(data_ref, ins[0] - 1) if ins[0] > 0 else None
    for span in ins:
        here = parts(data_ref, span)
        if before is None:
            own[span] = here if sign > 0 else tuple(-part for part in here)
        elif sign > 0:
            own[span] = tuple(b + h for b, h in zip(before, here))
        else:
            own[span] = tuple(b - h for b, h in zip(before, here))
        before = here
    for out in outs:
        first = second = cross = None
        for span in ins:
            if not 0 <= out - span < lags:
                continue
            (tr, ti), (xr, xi) = taps[out - span], own[span]
            if first is None:
                first, second, cross = tr * xr, ti * xi, tr * xi + ti * xr
            else:
                first, second = first + tr * xr, second + ti * xi
                cross = cross + tr * xi + ti * xr
        cols = slice((out % 2) * share, (out % 2 + 1) * share)
        if first is None:
            if not add:
                total_ref[out // 2, real_rows, cols] = jnp.zeros((ROWS, share), F32)
                total_ref[out // 2, imag_rows, cols] = jnp.zeros((ROWS, share), F32)
            continue
        real, imag = first - second, cross
        if edge:
            at_edge = lax.broadcasted_iota(jnp.int32, real.shape, 0) == 0
            real, imag = jnp.where(at_edge, first, real), jnp.where(at_edge, second, imag)
        if add:
            real += total_ref[out // 2, real_rows, cols]
            imag += total_ref[out // 2, imag_rows, cols]
        total_ref[out // 2, real_rows, cols] = real
        total_ref[out // 2, imag_rows, cols] = imag


def spectral_sums(outs, ins, add, taps_ref, data_ref, total_ref):
    refs = (taps_ref, data_ref, total_ref)
    tiles = data_ref.shape[1] // 4 // ROWS
    spectral_tile(0, 1, True, outs, ins, add, *refs)

    def even(i, carry):
        spectral_tile(pl.multiple_of(i * ROWS, ROWS), 1, False, outs, ins, add, *refs)
        return carry

    def odd(i, carry):
        spectral_tile(pl.multiple_of(i * ROWS, ROWS), -1, False, outs, ins, add, *refs)
        return carry

    lax.fori_loop(1, tiles, even, 0)
    lax.fori_loop(tiles, 2 * tiles, odd, 0)


def chunk_rows(length):
    ends = np.cumsum((0,) + EIGHTHS) * (length // 8)
    return [slice(int(a), int(b)) for a, b in zip(ends[:-1], ends[1:])]


def fused_kernel(
    n, q_hbm, k_hbm, v_hbm, taps_hbm, skip_ref, w_hbm, fwd_hbm, inv_hbm, out_ref,
    q_ref, k_ref, v_ref, taps_ref, w_ref, fwd_ref, inv_ref,
    mixed, recv1, spec_b, spec_x, total, total_b, send2, recv2, gated, s1, r1, s2, r2, acc,
    load_sem, own1_sem, own2_sem, a_send, a_recv, b_send, b_recv, c_send, c_recv, d_send, d_recv,
):
    me, ch = lax.axis_index("ctx"), lax.axis_index("ch")
    y, core = ch // 2, ch % 2
    beside, across = y * 2 + 1 - core, (1 - y) * 2 + core
    opposite = (1 - y) * 2 + 1 - core
    length, width = q_hbm.shape
    share, group = width // n, n // 2
    chunks = chunk_rows(length)
    side = me // group
    here = [side * group + lax.rem(me + i, group) for i in range(group)]
    there = [(1 - side) * group + lax.rem(me + i, group) for i in range(group)]
    order = [there[0]]
    for i in range(1, group):
        order += [here[i], there[i]]

    def load(index, src, dst):
        copy = pltpu.make_async_copy(src, dst, load_sem.at[index])
        copy.start()
        return copy

    taps_cols = pl.ds(pl.multiple_of(me * share, share), share)
    load_k, load_v = load(0, k_hbm, k_ref), load(1, v_hbm, v_ref)

    barrier = pltpu.get_barrier_semaphore()
    for peer in order:
        pl.semaphore_signal(barrier, inc=1, device_id={"ctx": peer}, device_id_type=MESH)
    for other in (beside, across):
        pl.semaphore_signal(barrier, inc=1, device_id={"ch": other}, device_id_type=MESH)

    load_k.wait()
    load_v.wait()
    load_fwd = load(2, fwd_hbm, fwd_ref)
    load_taps = load(3, taps_hbm.at[:, taps_cols], taps_ref)
    load_inv = load(4, inv_hbm, inv_ref)
    for d in range(n):
        cols = slice(d * share, (d + 1) * share)
        mixed[d] = (k_ref[:, cols].astype(F32) * v_ref[:, cols].astype(F32)).astype(BF16)
    pl.semaphore_wait(barrier, n + 1)

    def half(index):
        return pl.ds(pl.multiple_of(lax.rem(index, 2) * share, share), share)

    sends = []
    for i, peer in enumerate(order):
        copy = pltpu.make_async_remote_copy(
            src_ref=mixed.at[peer],
            dst_ref=recv1.at[me // 2, :, half(me)],
            send_sem=a_send.at[i],
            recv_sem=a_recv.at[me],
            device_id={"ctx": peer},
            device_id_type=MESH,
        )
        copy.start()
        sends.append(copy)
    own = pltpu.make_async_copy(mixed.at[me], recv1.at[me // 2, :, half(me)], own1_sem)
    own.start()
    load_q = load(5, q_hbm, q_ref)
    load_w = [
        load(6 + i, w_hbm.at[:, pl.ds(pl.multiple_of(owner * width, width), width)], w_ref.at[i])
        for i, owner in enumerate((opposite, beside, across, ch))
    ]

    load_fwd.wait()
    load_taps.wait()
    for p in range(spec_b.shape[0]):
        blocks = [taps_ref[(2 * p + i) * length : (2 * p + i + 1) * length] for i in range(2)]
        spec_b[p] = jnp.dot(
            fwd_ref[...], jnp.concatenate(blocks, axis=1).astype(BF16), preferred_element_type=F32
        )
    own.wait()

    def spectrum(p):
        for src in (2 * p, 2 * p + 1):

            @pl.when(src != me)
            def _():
                cols = slice((src % 2) * share, (src % 2 + 1) * share)
                pltpu.make_async_remote_copy(
                    src_ref=mixed.at[src],
                    dst_ref=recv1.at[src // 2, :, cols],
                    send_sem=a_send.at[0],
                    recv_sem=a_recv.at[src],
                    device_id={"ctx": order[0]},
                    device_id_type=MESH,
                ).wait_recv()

        spec_x[p] = jnp.dot(fwd_ref[...], recv1[p], preferred_element_type=F32)

    def way_back(t, peer):
        return pltpu.make_async_remote_copy(
            src_ref=send2.at[peer, chunks[t]],
            dst_ref=recv2.at[chunks[t], taps_cols],
            send_sem=b_send.at[t, peer],
            recv_sem=b_recv.at[t, me],
            device_id={"ctx": peer},
            device_id_type=MESH,
        )

    def own_rows(t):
        return pltpu.make_async_copy(
            send2.at[me, chunks[t]], recv2.at[chunks[t], taps_cols], own2_sem.at[t]
        )

    def launch(t, which):
        @pl.when(side == which)
        def _():
            own_rows(t).start()

        @pl.when(side != which)
        def _():
            way_back(t, which * group + lax.rem(me, group)).start()

        for i in range(1, group):
            way_back(t, which * group + lax.rem(me + i, group)).start()

    def send_back(which):
        pairs = range(which * group // 2, (which + 1) * group // 2)
        for p in pairs:
            total_b[p] = total[p].astype(BF16)
        for t, rows in enumerate(chunks):
            for p in pairs:
                conv = jnp.dot(inv_ref[rows], total_b[p], preferred_element_type=F32).astype(BF16)
                send2[2 * p, rows] = conv[:, :share]
                send2[2 * p + 1, rows] = conv[:, share:]
            if t < AHEAD:
                launch(t, which)

    low, high = range(group), range(group, n)
    for p in range(group // 2):
        spectrum(p)
    spectral_sums(low, low, False, spec_b, spec_x, total)
    load_inv.wait()
    send_back(0)
    spectral_sums(high, low, False, spec_b, spec_x, total)
    for p in range(group // 2, group):
        spectrum(p)
    spectral_sums(high, high, True, spec_b, spec_x, total)
    send_back(1)

    def exchange(src, dst, out_sem, in_sem, other):
        copy = pltpu.make_async_remote_copy(
            src_ref=src,
            dst_ref=dst,
            send_sem=out_sem,
            recv_sem=in_sem,
            device_id={"ch": other},
            device_id_type=MESH,
        )
        copy.start()
        sends.append(copy)
        return copy

    def project(rows, block):
        return jnp.dot(gated[rows], w_ref[block], preferred_element_type=F32)

    def finish(t, copy):
        copy.wait_recv()
        out_ref[chunks[t]] = (acc[chunks[t]] + r2[chunks[t]].astype(F32)).astype(BF16)

    load_q.wait()
    for copy in load_w:
        copy.wait()
    last = None
    for t, rows in enumerate(chunks):
        own_rows(t).wait()
        for src in range(n):

            @pl.when(src != me)
            def _():
                cols = slice(src * share, (src + 1) * share)
                pltpu.make_async_remote_copy(
                    src_ref=send2.at[src, rows],
                    dst_ref=recv2.at[rows, cols],
                    send_sem=b_send.at[t, src],
                    recv_sem=b_recv.at[t, src],
                    device_id={"ctx": order[0]},
                    device_id_type=MESH,
                ).wait_recv()

        for d in range(n):
            cols = slice(d * share, (d + 1) * share)
            conv = recv2[rows, cols].astype(F32)
            conv = conv + skip_ref[:, cols] * mixed[d, rows].astype(F32)
            gated[rows, cols] = (q_ref[rows, cols].astype(F32) * conv).astype(BF16)
        s1[0, rows] = project(rows, 0).astype(BF16)
        far = exchange(s1.at[0, rows], r1.at[0, rows], c_send.at[t, 0], c_recv.at[t, 0], beside)
        s1[1, rows] = project(rows, 1).astype(BF16)
        near = exchange(s1.at[1, rows], r1.at[1, rows], c_send.at[t, 1], c_recv.at[t, 1], beside)
        if t + AHEAD < len(chunks):
            launch(t + AHEAD, 0)
            launch(t + AHEAD, 1)
        passed = project(rows, 2)
        far.wait_recv()
        s2[rows] = (passed + r1[0, rows].astype(F32)).astype(BF16)
        final = exchange(s2.at[rows], r2.at[rows], d_send.at[t], d_recv.at[t], across)
        kept = project(rows, 3)
        near.wait_recv()
        acc[rows] = kept + r1[1, rows].astype(F32)
        if last is not None:
            finish(t - 1, last)
        last = final
    finish(len(chunks) - 1, last)
    for copy in sends:
        copy.wait_send()
    for t in range(len(chunks)):
        for i in range(1, group):
            way_back(t, here[i]).wait_send()
        for peer in there:
            way_back(t, peer).wait_send()


def fused_body(forward, inverse, query_gate, key_gate, value_in, filter_taps, skip_gain, out_weight):
    length, width = query_gate.shape
    n = lax.axis_size("ctx")
    share, taps, chunks = width // n, filter_taps.shape[0], len(EIGHTHS)
    dma = pltpu.SemaphoreType.DMA
    anywhere = pl.BlockSpec(memory_space=pl.ANY)
    vmem = pl.BlockSpec(memory_space=pltpu.VMEM)
    return pl.pallas_call(
        functools.partial(fused_kernel, n),
        out_shape=jax.ShapeDtypeStruct((length, width), BF16),
        in_specs=[anywhere] * 4 + [vmem] + [anywhere] * 3,
        out_specs=vmem,
        scratch_shapes=[
            pltpu.VMEM((length, width), BF16),
            pltpu.VMEM((length, width), BF16),
            pltpu.VMEM((length, width), BF16),
            pltpu.VMEM((taps, share), F32),
            pltpu.VMEM((4, width, width), BF16),
            pltpu.VMEM((2 * length, length), BF16),
            pltpu.VMEM((length, 2 * length), BF16),
            pltpu.VMEM((n, length, share), BF16),
            pltpu.VMEM((n // 2, length, 2 * share), BF16),
            pltpu.VMEM((taps // length // 2, 2 * length, 2 * share), F32),
            pltpu.VMEM((n // 2, 2 * length, 2 * share), F32),
            pltpu.VMEM((n // 2, 2 * length, 2 * share), F32),
            pltpu.VMEM((n // 2, 2 * length, 2 * share), BF16),
            pltpu.VMEM((n, length, share), BF16),
            pltpu.VMEM((length, width), BF16),
            pltpu.VMEM((length, width), BF16),
            pltpu.VMEM((2, length, width), BF16),
            pltpu.VMEM((2, length, width), BF16),
            pltpu.VMEM((length, width), BF16),
            pltpu.VMEM((length, width), BF16),
            pltpu.VMEM((length, width), F32),
            dma((10,)),
            dma,
            dma((chunks,)),
            dma((n - 1,)),
            dma((n,)),
            dma((chunks, n)),
            dma((chunks, n)),
            dma((chunks, 2)),
            dma((chunks, 2)),
            dma((chunks,)),
            dma((chunks,)),
        ],
        compiler_params=pltpu.CompilerParams(
            collective_id=0, has_side_effects=True, vmem_limit_bytes=56 * 2**20
        ),
        cost_estimate=pl.CostEstimate(
            flops=10 * 10**9, bytes_accessed=16 * 2**20, transcendentals=0
        ),
    )(
        query_gate, key_gate, value_in, filter_taps, skip_gain.reshape(1, width), out_weight,
        forward, inverse,
    )


def solution(mesh):
    in_specs = (
        P("ctx", "ch"),
        P("ctx", "ch"),
        P("ctx", "ch"),
        P(None, "ch"),
        P("ch"),
        P("ch", None),
    )
    out_specs = P("ctx", "ch")

    def whole(query_gate, *rest):
        length = query_gate.shape[0] // mesh.shape["ctx"]
        width = query_gate.shape[1] // mesh.shape["ch"]
        forward, inverse = transform_tables(length)
        taps = rest[2].shape[0] // length
        fits = mesh.shape["ch"] == 4 and width == 128 * mesh.shape["ctx"]
        fits = fits and mesh.shape["ctx"] % 4 == 0 and taps % 2 == 0 and length % 128 == 0
        chosen = fused_body if fits else plain_body

        def body(*args):
            return chosen(jnp.asarray(forward), jnp.asarray(inverse), *args)

        return jax.shard_map(
            body, mesh=mesh, in_specs=in_specs, out_specs=out_specs, check_vma=False
        )(query_gate, *rest)

    return whole
```
